32 devices in a mesh: dp: 2 (over core), wide: 16 (over z, y, x).
Axes of the slice: x: 2, y: 2, z: 4, core: 2. Of those that a mesh axis runs over, the one named last changes fastest.
Arguments:
- tokens: bfloat16 [114688, 128], P(('dp', 'wide')), may hold values from -6 to 6
- field_ids: int32 [114688], P(('dp', 'wide')), may hold values from 0 to 3
- seq_lengths: int32 [224], P(('dp', 'wide')), may hold values from 128 to 512, as said below
- cotangent: bfloat16 [114688, 128], P(('dp', 'wide')), may hold values from -6 to 6
- attn_weight: bfloat16 [2, 128, 384], P(None, 'wide'), may hold values from -0.5 to 0.5
- query_bias: bfloat16 [2, 128], P(None, 'wide'), may hold values from -3 to 3
- value_bias: bfloat16 [2, 128], P(None, 'wide'), may hold values from -3 to 3
- proj_weight: bfloat16 [2, 128, 128], P(None, 'wide'), may hold values from -4 to 4
- proj_bias: bfloat16 [2, 128], P(None, 'wide'), may hold values from -3 to 3
- attn_gain: bfloat16 [2, 128], P(None, 'wide'), may hold values from 0.5 to 1.5
- attn_shift: bfloat16 [2, 128], P(None, 'wide'), may hold values from -3 to 3
- up_weight: bfloat16 [2, 128, 512], P(None, 'wide'), may hold values from -0.5 to 0.5
- up_bias: bfloat16 [2, 512], P(None, 'wide'), may hold values from -3 to 3
- down_weight: bfloat16 [2, 512, 128], P(None, 'wide'), may hold values from -0.25 to 0.25
- down_bias: bfloat16 [2, 128], P(None, 'wide'), may hold values from -3 to 3
- ffn_gain: bfloat16 [2, 128], P(None, 'wide'), may hold values from 0.5 to 1.5
- ffn_shift: bfloat16 [2, 128], P(None, 'wide'), may hold values from -3 to 3
Outputs:
- output: bfloat16 [114688, 128], P(('dp', 'wide'))
- token_grad: float32 [114688, 128], P(('dp', 'wide'))
- attn_weight_grad: float32 [2, 128, 384], P(None, 'wide')
- query_bias_grad: float32 [2, 128], P(None, 'wide')
- value_bias_grad: float32 [2, 128], P(None, 'wide')
- proj_weight_grad: float32 [2, 128, 128], P(None, 'wide')
- proj_bias_grad: float32 [2, 128], P(None, 'wide')
- attn_gain_grad: float32 [2, 128], P(None, 'wide')
- attn_shift_grad: float32 [2, 128], P(None, 'wide')
- up_weight_grad: float32 [2, 128, 512], P(None, 'wide')
- up_bias_grad: float32 [2, 512], P(None, 'wide')
- down_weight_grad: float32 [2, 512, 128], P(None, 'wide')
- down_bias_grad: float32 [2, 128], P(None, 'wide')
- ffn_gain_grad: float32 [2, 128], P(None, 'wide')
- ffn_shift_grad: float32 [2, 128], P(None, 'wide')
The draws below stay inside these ranges and needn't reach their ends.
Inputs may be any that keep to these rules, and one draw needn't show every extreme that they name: `seq_lengths`: some sequence is 512 tokens long and some is a quarter of 512.
All inputs are finite; a program needn't handle non-finite values.
Results may differ from the reference program's by a relative error of at most 0.014.
Values may be sent and summed in bfloat16 or wider, within the bound.
No kernel may reach another device: no remote copies, remote signals or barrier semaphores. Data moves between devices by JAX's collectives and lax.ppermute only.
A program may use at most 128 MiB of HBM per device.

```python
import jax
import jax.numpy as jnp
from jax import lax

D = 128
HEADS = 4
FF = 512
L = 512
LAYERS = 2
SEQ_DEV = 7
SEQS = 224
TOKENS = 114688


def draw_seq_lengths(key, part):
    key = jax.random.fold_in(key, 7)
    key_values, key_long, key_short = jax.random.split(key, 3)
    values = jax.random.randint(key_values, (SEQS,), L // 4, L + 1)
    longest = jax.random.randint(key_long, (), 0, SEQS)
    shortest = (longest + 1 + jax.random.randint(key_short, (), 0, SEQS - 1)) % SEQS
    values = values.at[longest].set(L)
    values = values.at[shortest].set(L // 4)
    return values.astype(jnp.int32)


def set_ends(result, key, smallest, high):
    dims = result.shape
    index_at = [jax.random.randint(jax.random.fold_in(key, axis), (), 0, dims[axis]) for axis in range(len(dims))]
    result = result.at[tuple(index_at)].set(smallest)
    longest = dims.index(max(dims))
    index_at[longest] = (index_at[longest] + 1) % dims[longest]
    return result.at[tuple(index_at)].set(high)


def with_spikes(result, rng, source, target, parts, factor):
    owner, partner = [(jnp.arange(result.shape[dim]) // (result.shape[dim] // parts)).reshape([-1 if axis == dim else 1 for axis in range(result.ndim)]) for dim in (source, target)]
    chosen = jax.random.permutation(rng, parts)[partner]
    strong = (owner == chosen) | (owner == (partner + parts // 2) % parts)
    return jnp.where(strong, factor * result, result)


def levels(rng, extent, pieces, smallest, top_value):
    def one(position, shards_of):
        steps = jax.random.uniform(jax.random.fold_in(jax.random.fold_in(rng, 6), position), (shards_of,), jnp.float32, smallest / len(pieces), top_value / len(pieces))
        return jnp.repeat(jnp.exp(steps), extent[position] // shards_of).reshape((-1,) + (1,) * (len(extent) - position - 1))

    factor_of = one(*pieces[0])
    for cut in pieces[1:]:
        factor_of = factor_of * one(*cut)
    return factor_of


def scatter_about(stream_key, shape, scale, most, pieces=(), dtype=jnp.bfloat16):
    entries = jax.random.normal(stream_key, shape, jnp.float32) * scale
    if len(pieces) > 0:
        entries = levels(stream_key, shape, pieces, -0.22, 0.18) * entries
    return jnp.clip(entries, min=-most, max=most).astype(dtype)


def heavy_noise(stream_key, extent, width, most, cuts, heavy, held_as=jnp.bfloat16):
    array = width * jax.random.normal(stream_key, extent, jnp.float32)
    if cuts:
        array = array * levels(stream_key, extent, cuts, -0.22, 0.18)
    return jnp.clip(with_spikes(array, jax.random.fold_in(stream_key, 3), *heavy), -most, most).astype(held_as)


def setup_inputs(seed: int = 0) -> dict:
    streams_of = jax.random.split(jax.random.key(seed), 18)
    tokens = scatter_about(streams_of[0], (TOKENS, D), 1.0, 6.0, ((0, 32),))
    field_ids = set_ends(jax.random.randint(streams_of[1], (TOKENS,), 0, 4), jax.random.fold_in(streams_of[1], 1), 0, 3).astype(jnp.int32)
    seq_lengths = draw_seq_lengths(jax.random.fold_in(streams_of[17], 71), 0)
    cotangent = heavy_noise(streams_of[3], (TOKENS, D), 1.0, 6.0, ((0, 32),), (0, 1, 32, 2.75))
    attn_weight = scatter_about(streams_of[4], (LAYERS, D, 3 * D), D ** -0.5, 0.5, ((1, 16),))
    query_bias = scatter_about(streams_of[5], (LAYERS, D), 0.5, 3.0, ((1, 16),))
    value_bias = scatter_about(streams_of[6], (LAYERS, D), 0.5, 3.0, ((1, 16),))
    proj_weight = scatter_about(streams_of[7], (LAYERS, D, D), (D // 64) ** -0.5, 4.0, ((1, 16),))
    proj_bias = scatter_about(streams_of[8], (LAYERS, D), 0.5, 3.0, ((1, 16),))
    attn_gain = jnp.clip(1.0 + 0.1 * jax.random.normal(streams_of[9], (LAYERS, D), jnp.float32), 0.5, 1.5).astype(jnp.bfloat16)
    attn_shift = scatter_about(streams_of[10], (LAYERS, D), 0.5, 3.0, ((1, 16),))
    up_weight = scatter_about(streams_of[11], (LAYERS, D, FF), D ** -0.5, 0.5, ((1, 16),))
    up_bias = scatter_about(streams_of[12], (LAYERS, FF), 0.5, 3.0, ((1, 16),))
    down_weight = scatter_about(streams_of[13], (LAYERS, FF, D), FF ** -0.5, 0.25, ((1, 16),))
    down_bias = scatter_about(streams_of[14], (LAYERS, D), 0.5, 3.0, ((1, 16),))
    ffn_gain = jnp.clip(1.0 + 0.1 * jax.random.normal(streams_of[15], (LAYERS, D), jnp.float32), 0.5, 1.5).astype(jnp.bfloat16)
    ffn_shift = scatter_about(streams_of[16], (LAYERS, D), 0.5, 3.0, ((1, 16),))
    return {"tokens": tokens, "field_ids": field_ids, "seq_lengths": seq_lengths, "cotangent": cotangent, "attn_weight": attn_weight, "query_bias": query_bias, "value_bias": value_bias, "proj_weight": proj_weight, "proj_bias": proj_bias, "attn_gain": attn_gain, "attn_shift": attn_shift, "up_weight": up_weight, "up_bias": up_bias, "down_weight": down_weight, "down_bias": down_bias, "ffn_gain": ffn_gain, "ffn_shift": ffn_shift}


@jax.custom_vjp
def low(v):
    return lax.optimization_barrier(v.astype(jnp.bfloat16)).astype(jnp.float32)

@jax.custom_vjp
def low_back(v):
    return v

def low_keep(v):
    return (low(v), None)

def low_pass(kept, grad):
    return (grad,)

def back_keep(v):
    return (v, None)

def back_low(kept, grad):
    return (low(grad),)
low.defvjp(low_keep, low_pass)
low_back.defvjp(back_keep, back_low)
EPSILON = 1e-05
NEGATIVE = -1e+30
PRECISE = lax.Precision.HIGHEST

def normalize(hidden, gain_row, shift_row):
    centre = lax.optimization_barrier(jnp.mean(hidden, axis=-1, keepdims=True))
    centred = hidden - centre
    spread = lax.optimization_barrier(jnp.mean(centred * centred, axis=-1, keepdims=True))
    return centred * lax.rsqrt(spread + EPSILON) * gain_row + shift_row

def visible(field_rows, valid_lengths):
    seq_length = field_rows.shape[-1]
    row_index = jnp.arange(seq_length)[:, None]
    col_index = jnp.arange(seq_length)[None, :]
    open_keys = (col_index[None] < valid_lengths[:, None, None]) & (field_rows[:, None, :] != 0)
    return (row_index == col_index)[None] | (col_index < row_index)[None] & open_keys

def block(hidden, params, keep_mask):
    attn_weight, query_bias, value_bias, proj_weight, proj_bias, attn_gain, attn_shift, up_weight, up_bias, down_weight, down_bias, ffn_gain, ffn_shift = params
    feature_width = hidden.shape[-1]
    head_size = feature_width // HEADS
    split_shape = hidden.shape[:2] + (HEADS, head_size)
    normed = low(normalize(hidden, attn_gain, attn_shift))
    packed = jnp.einsum('gld,de->gle', normed, attn_weight, precision=PRECISE)
    queries = low_back(low(packed[..., :feature_width] + query_bias))
    keys_all = low_back(low(packed[..., feature_width:2 * feature_width]))
    values_all = low_back(low(packed[..., 2 * feature_width:] + value_bias))
    scores = jnp.einsum('gqhd,gkhd->ghqk', queries.reshape(split_shape), keys_all.reshape(split_shape), precision=PRECISE) * head_size ** (-0.5)
    scores = jnp.where(keep_mask[:, None], low_back(scores), NEGATIVE)
    probs_low = low(jax.nn.softmax(scores, axis=-1))
    attended = jnp.einsum('ghqk,gkhd->gqhd', probs_low, values_all.reshape(split_shape), precision=PRECISE).reshape(hidden.shape)
    attended = low_back(low(attended))
    branch_one = low_back(jnp.einsum('gld,de->gle', attended, proj_weight, precision=PRECISE) + proj_bias)
    middle = hidden + branch_one
    normed_two = low(normalize(middle, ffn_gain, ffn_shift))
    expanded = low_back(jnp.einsum('gld,df->glf', normed_two, up_weight, precision=PRECISE) + up_bias)
    activated = low(jax.nn.gelu(expanded))
    branch_two = low_back(jnp.einsum('glf,fd->gld', activated, down_weight, precision=PRECISE) + down_bias)
    return middle + branch_two

def reference(tokens, field_ids, seq_lengths, cotangent, attn_weight, query_bias, value_bias, proj_weight, proj_bias, attn_gain, attn_shift, up_weight, up_bias, down_weight, down_bias, ffn_gain, ffn_shift):
    params = tuple((weight_arg.astype(jnp.float32) for weight_arg in (attn_weight, query_bias, value_bias, proj_weight, proj_bias, attn_gain, attn_shift, up_weight, up_bias, down_weight, down_bias, ffn_gain, ffn_shift)))
    group_count = tokens.shape[0] // (SEQ_DEV * L)
    group_shape = (group_count, SEQ_DEV, L, D)
    batches = (tokens.astype(jnp.float32).reshape(group_shape), cotangent.astype(jnp.float32).reshape(group_shape), field_ids.reshape(group_count, SEQ_DEV, L), seq_lengths.reshape(group_count, SEQ_DEV))

    def forward(hidden, weight_set, keep_mask):
        for layer_index in range(LAYERS):
            hidden = block(hidden, tuple((entry[layer_index] for entry in weight_set)), keep_mask)
        return hidden

    def visit(running, batch):
        inputs_group, cot_group, field_group, length_group = batch
        keep_mask = visible(field_group, length_group)
        outputs_group, pullback = jax.vjp(lambda hidden, weight_set: forward(hidden, weight_set, keep_mask), inputs_group, params)
        input_grad, weight_grads = pullback(cot_group)
        return (tuple((total_now + addend for total_now, addend in zip(running, weight_grads))), (outputs_group, input_grad))
    zeros_init = tuple((jnp.zeros_like(weight_arg) for weight_arg in params))
    totals, (outputs_all, grads_all) = lax.scan(visit, zeros_init, batches)
    return (outputs_all.reshape(-1, D).astype(jnp.bfloat16), grads_all.reshape(-1, D), totals[0], totals[1], totals[2], totals[3], totals[4], totals[5], totals[6], totals[7], totals[8], totals[9], totals[10], totals[11], totals[12])
```

```python
import functools
import math

import jax
import jax.numpy as jnp
from jax import lax
from jax.experimental import pallas as pl
from jax.experimental.pallas import tpu as pltpu
from jax.sharding import PartitionSpec as P

HEADS = 4
EPSILON = 1e-05
NEGATIVE = -1e30
BLOCK = 128
D = 128
FF = 512
OWNERS = 16
SHARD_ROWS = 104
GRAD_ROWS = 112
LAYERS = 2
GROUP = 2
VMEM_BYTES = 60 * 2**20

BF = jnp.bfloat16
F32 = jnp.float32
NN = (((1,), (0,)), ((), ()))


def dot(a, b):
    return lax.dot_general(a, b, NN, preferred_element_type=F32)


def flip(x):
    return jnp.transpose(x)


def col(vec_ref, index):
    return vec_ref[:, index : index + 1]


def reverse_bits(x):
    return ((x & 1) << 3) | ((x & 2) << 1) | ((x & 4) >> 1) | ((x & 8) >> 3)


def unpack(me, packed_ref, stage):
    place = reverse_bits(me)
    for owner in range(OWNERS):
        stage[owner] = packed_ref[jnp.bitwise_xor(place, reverse_bits(owner))].astype(F32)


def stage_rows(stage, start, count):
    return stage[:, start : start + count, :].reshape(OWNERS * count, 128)


def unpack_forward(stage, qkv_t, proj_t, up_t, down_t):
    for part in range(3):
        qkv_t[part * D : (part + 1) * D, :] = flip(stage_rows(stage, 8 * part, 8)).astype(BF)
    proj_t[...] = flip(stage_rows(stage, 24, 8)).astype(BF)
    for part in range(4):
        up_t[part * D : (part + 1) * D, :] = flip(stage_rows(stage, 32 + 8 * part, 8)).astype(BF)
    down_t[...] = flip(stage_rows(stage, 64, 32)).astype(BF)


def unpack_backward(stage, qkv, proj, up, down):
    for part in range(3):
        qkv[:, part * D : (part + 1) * D] = stage_rows(stage, 8 * part, 8).astype(BF)
    proj[...] = stage_rows(stage, 24, 8).astype(BF)
    for part in range(4):
        up[:, part * D : (part + 1) * D] = stage_rows(stage, 32 + 8 * part, 8).astype(BF)
    down[...] = stage_rows(stage, 64, 32).astype(BF)


def unpack_vectors(stage, vec, up_bias):
    small = stage[:, 96:104, :]
    vec[...] = small.reshape(D, 128)
    for part in range(4):
        piece = small[:, :, 8 + part : 9 + part]
        up_bias[:, part, :, :] = jnp.broadcast_to(piece, (OWNERS, 8, 128))


QUERY_BIAS, VALUE_BIAS, PROJ_BIAS, ATTN_GAIN, ATTN_SHIFT, DOWN_BIAS, FFN_GAIN, FFN_SHIFT = range(8)


def norm_stats(x):
    mean = jnp.mean(x, axis=0, keepdims=True)
    centred = x - mean
    spread = jnp.mean(centred * centred, axis=0, keepdims=True)
    rstd = lax.rsqrt(spread + EPSILON)
    return centred * rstd, rstd


def norm_backward(grad_out, gain, unit, rstd):
    weighted = grad_out * gain
    first = jnp.mean(weighted, axis=0, keepdims=True)
    second = jnp.mean(weighted * unit, axis=0, keepdims=True)
    return rstd * (weighted - first - unit * second)


def head_columns(x, block):
    size = D // HEADS
    piece = x[:, block * BLOCK : (block + 1) * BLOCK]
    columns = []
    for head in range(HEADS):
        rows = [
            piece[head * size : (head + 1) * size] if other == head else jnp.zeros((size, BLOCK), piece.dtype)
            for other in range(HEADS)
        ]
        columns.append(jnp.concatenate(rows, axis=0))
    return jnp.concatenate(columns, axis=1)


def head_rows(x, block):
    size = D // HEADS
    piece = x[block * BLOCK : (block + 1) * BLOCK, :]
    lane = lax.broadcasted_iota(jnp.int32, (BLOCK, D), 1) // size
    return jnp.concatenate(
        [jnp.where(lane == head, piece, jnp.zeros_like(piece)) for head in range(HEADS)], axis=0
    )


def head_diagonal(x):
    size = D // HEADS
    return jnp.concatenate(
        [x[head * size : (head + 1) * size, head * BLOCK : (head + 1) * BLOCK] for head in range(HEADS)], axis=0
    )


def head_spread(rows):
    size = D // HEADS
    return jnp.concatenate(
        [jnp.broadcast_to(rows[head : head + 1], (size, rows.shape[1])) for head in range(HEADS)], axis=0
    )


def extra_rows(rows, total=D):
    width = rows[0].shape[1]
    filled = jnp.zeros((16, width), F32)
    place = lax.broadcasted_iota(jnp.int32, (16, width), 0)
    for index, row in enumerate(rows):
        filled = jnp.where(place == index, jnp.broadcast_to(row, (16, width)), filled)
    return jnp.concatenate([filled.astype(BF), jnp.zeros((total - 16, width), BF)], axis=0)


def layer_forward(x, key_bias, w, save):
    qkv_t, proj_t, up_t, down_t, vec, up_bias = w
    tokens = x.shape[1]
    blocks = tokens // BLOCK
    size = D // HEADS
    unit, rstd = norm_stats(x)
    normed = (unit * col(vec, ATTN_GAIN) + col(vec, ATTN_SHIFT)).astype(BF)
    save["unit"][...] = unit.astype(BF)
    yield
    packed = dot(qkv_t[...], normed)
    factor = size ** (-0.5) / math.log(2.0)
    query = ((packed[:D] + col(vec, QUERY_BIAS)) * factor).astype(BF)
    key = packed[D : 2 * D].astype(BF)
    value = (packed[2 * D :] + col(vec, VALUE_BIAS)).astype(BF)
    save["query"][...] = query
    save["key"][...] = key
    save["value"][...] = value
    key_rows = jnp.concatenate([flip(key), key_bias], axis=1)
    product = query.astype(F32) * key.astype(F32)
    own = [jnp.sum(product[h * size : (h + 1) * size], axis=0, keepdims=True) for h in range(HEADS)]
    value_ones = jnp.concatenate([value, jnp.ones((16, tokens), BF)], axis=0)
    ones = extra_rows([jnp.ones((1, HEADS * BLOCK), F32)])
    key_at = lax.broadcasted_iota(jnp.int32, (BLOCK, HEADS * BLOCK), 0)
    query_at = lax.broadcasted_iota(jnp.int32, (BLOCK, HEADS * BLOCK), 1) % BLOCK
    attended, inverse = [], []
    for block in range(blocks):
        yield
        seen = (block + 1) * BLOCK
        right = jnp.concatenate([head_columns(query, block), ones], axis=0)
        scores = dot(key_rows[:seen], right)
        own_row = jnp.concatenate([o[:, block * BLOCK : seen] for o in own], axis=1)
        last = scores[seen - BLOCK :]
        last = jnp.where(key_at < query_at, last, NEGATIVE)
        last = jnp.where(key_at == query_at, jnp.broadcast_to(own_row, last.shape), last)
        if block:
            scores = jnp.concatenate([scores[: seen - BLOCK], last], axis=0)
        else:
            scores = last
        yield
        highest = jnp.max(scores, axis=0, keepdims=True)
        raised = jnp.exp2(scores - highest).astype(BF)
        save["probs"][block][...] = raised
        yield
        summed = dot(value_ones[:, :seen], raised)
        total = summed[D : D + 1]
        inv = 1.0 / total
        inverse.append(
            jnp.concatenate([inv[:, h * BLOCK : (h + 1) * BLOCK] for h in range(HEADS)], axis=0)
        )
        attended.append(head_diagonal(summed[:D] * inv))
    attended = jnp.concatenate(attended, axis=1)
    inverse = jnp.concatenate(inverse, axis=1)
    save["attended"][...] = attended
    yield
    middle = x + (dot(proj_t[...], attended.astype(BF)) + col(vec, PROJ_BIAS))
    unit_two, rstd_two = norm_stats(middle)
    save["unit_two"][...] = unit_two.astype(BF)
    save["rows"][...] = jnp.concatenate(
        [rstd, rstd_two, inverse, jnp.zeros((2, tokens), F32)], axis=0
    )
    normed_two = (unit_two * col(vec, FFN_GAIN) + col(vec, FFN_SHIFT)).astype(BF)
    result = middle + col(vec, DOWN_BIAS)
    chunk = 256
    for start in range(0, FF, chunk):
        yield
        bias = up_bias[start : start + chunk]
        expanded = dot(up_t[start : start + chunk], normed_two) + jnp.concatenate(
            [bias] * (tokens // 128), axis=1
        )
        square = expanded * expanded
        root = math.sqrt(2.0 / math.pi)
        bent = jnp.tanh(expanded * (root + root * 0.044715 * square))
        half = 0.5 + 0.5 * bent
        yield
        active = (expanded * half).astype(BF)
        slope = half + (0.5 * expanded) * (1.0 - bent * bent) * (root + 3 * root * 0.044715 * square)
        save["active"][start : start + chunk] = active
        save["slope"][start : start + chunk] = slope.astype(BF)
        result = result + dot(down_t[:, start : start + chunk], active)
    return result


def layer_backward(grad, grad_rows, w, kept, total):
    qkv, proj, up, down, vec = w
    tokens = grad.shape[1]
    blocks = tokens // BLOCK
    size = D // HEADS
    grad_low = grad.astype(BF)
    unit_two = kept["unit_two"][...]
    ones_row = jnp.ones((16, tokens), BF)
    lane = lax.broadcasted_iota(jnp.int32, (tokens, D), 1)
    ones_lane = jnp.where(lane == 0, 1.0, 0.0).astype(BF)
    unit_two_rows = jnp.concatenate([flip(unit_two), ones_lane], axis=1)
    chunk = 256
    grad_normed = None
    for start in range(0, FF, chunk):
        yield
        active = kept["active"][start : start + chunk]
        total["down"][start : start + chunk] += dot(active, grad_rows)
        grad_active = dot(down[start : start + chunk], grad_low)
        grad_exp = (grad_active * kept["slope"][start : start + chunk].astype(F32)).astype(BF)
        yield
        total["up"][start : start + chunk] += dot(grad_exp, unit_two_rows)
        part = dot(up[:, start : start + chunk], grad_exp)
        grad_normed = part if grad_normed is None else grad_normed + part
    total["down_bias"][...] += dot(ones_row, grad_rows)[:8]
    yield
    rows = kept["rows"][...]
    grad_middle = grad + norm_backward(
        grad_normed, col(vec, FFN_GAIN), unit_two.astype(F32), rows[1:2]
    )
    grad_proj = grad_middle.astype(BF)
    grad_proj_rows = flip(grad_proj)
    attended = kept["attended"][...]
    total["proj"][...] += dot(jnp.concatenate([attended.astype(BF), ones_row], axis=0), grad_proj_rows)
    yield
    grad_attended = dot(proj[...], grad_proj).astype(BF).astype(F32)
    scaled = (grad_attended * head_spread(rows[2 : 2 + HEADS])).astype(BF)
    product = scaled.astype(F32) * attended
    centre = [jnp.sum(product[h * size : (h + 1) * size], axis=0, keepdims=True) for h in range(HEADS)]
    centre_high = [c.astype(BF).astype(F32) for c in centre]
    centre_low = [c - high for c, high in zip(centre, centre_high)]
    minus = jnp.where(lane < 2, -1.0, 0.0).astype(BF)
    value_rows = jnp.concatenate([flip(kept["value"][...]), minus], axis=1)
    key = kept["key"][...]
    query_rows = flip(kept["query"][...])
    scaled_rows = flip(scaled)
    grad_query = []
    grad_value = [None] * blocks
    grad_key = [None] * blocks

    def gather_row(parts, block):
        return jnp.concatenate([p[:, block * BLOCK : (block + 1) * BLOCK] for p in parts], axis=1)

    for block in range(blocks):
        yield
        seen = (block + 1) * BLOCK
        right = jnp.concatenate(
            [
                head_columns(scaled, block),
                extra_rows([gather_row(centre_high, block), gather_row(centre_low, block)]),
            ],
            axis=0,
        )
        grad_probs = dot(value_rows[:seen], right)
        raised = kept["probs"][block][...]
        grad_scores = raised * grad_probs.astype(BF)
        yield
        grad_query.append(head_diagonal(dot(key[:, :seen], grad_scores)))
        value_part = dot(raised, head_rows(scaled_rows, block))
        key_part = dot(grad_scores, head_rows(query_rows, block))
        for j in range(block + 1):
            v = value_part[j * BLOCK : (j + 1) * BLOCK]
            k = key_part[j * BLOCK : (j + 1) * BLOCK]
            grad_value[j] = v if grad_value[j] is None else grad_value[j] + v
            grad_key[j] = k if grad_key[j] is None else grad_key[j] + k
    yield
    grad_query = (jnp.concatenate(grad_query, axis=1) * size ** (-0.5)).astype(BF)
    grad_key = (jnp.concatenate(grad_key, axis=0) * math.log(2.0)).astype(BF)
    grad_value = jnp.concatenate(grad_value, axis=0).astype(BF)
    packed_rows = jnp.concatenate([flip(grad_query), grad_key, grad_value], axis=1)
    packed = jnp.concatenate([grad_query, flip(grad_key), flip(grad_value)], axis=0)
    unit = kept["unit"][...]
    total["qkv"][...] += dot(jnp.concatenate([unit, ones_row], axis=0), packed_rows)
    yield
    grad_normed = dot(qkv[...], packed)
    return grad_middle + norm_backward(
        grad_normed, col(vec, ATTN_GAIN), unit.astype(F32), rows[0:1]
    )


def pack_grads(me, total, send):
    place = reverse_bits(me)
    qkv, proj, up, down, down_bias = (total[n] for n in ("qkv", "proj", "up", "down", "down_bias"))
    up_t = [flip(up[D * part : D * (part + 1), :D]) for part in range(4)]
    up_sum = up[:, D:]
    up_sum_rows = [flip(up_sum[D * part : D * (part + 1)])[0:1] for part in range(4)]
    sums = jnp.concatenate(
        [
            qkv[D : D + 1, :D],
            qkv[D : D + 1, 2 * D : 3 * D],
            proj[D : D + 1],
            down_bias[0:1],
            jnp.zeros((D - 4, D), F32),
        ],
        axis=0,
    )
    columns = flip(sums)
    lane = lax.broadcasted_iota(jnp.int32, (8, 128), 1)
    whole = jnp.concatenate(
        [qkv[D : D + 1, D * part : D * (part + 1)] for part in range(3)]
        + up_sum_rows
        + [jnp.zeros((1, D), F32)],
        axis=0,
    )
    for owner in range(OWNERS):
        own = slice(8 * owner, 8 * owner + 8)
        small = jnp.where(lane < 4, columns[own], 0.0)
        for part in range(4):
            at = 32 * owner + 8 * part
            small = jnp.where(lane == 4 + part, jnp.broadcast_to(up_sum[at : at + 8, 0:1], (8, 128)), small)
        pieces = (
            [qkv[own, D * part : D * (part + 1)] for part in range(3)]
            + [proj[own]]
            + [u[own] for u in up_t]
            + [down[32 * owner : 32 * owner + 32], small, whole]
        )
        send[jnp.bitwise_xor(place, reverse_bits(owner))] = jnp.concatenate(pieces, axis=0).astype(BF)


KEPT = ("unit", "query", "key", "value", "attended", "unit_two", "rows", "active", "slope")


def kept_shapes(tokens):
    shapes = {name: ((D, tokens), BF) for name in KEPT}
    shapes["rows"] = ((8, tokens), F32)
    shapes["attended"] = ((D, tokens), F32)
    shapes["active"] = ((FF, tokens), BF)
    shapes["slope"] = ((FF, tokens), BF)
    for block in range(tokens // BLOCK):
        shapes[f"probs{block}"] = (((block + 1) * BLOCK, HEADS * BLOCK), BF)
    return shapes


def as_kept(names, refs):
    kept = dict(zip(names, refs))
    probs = [kept.pop(n) for n in names if n.startswith("probs")]
    kept["probs"] = probs
    return kept


FORWARD_SCRATCH = [
    pltpu.VMEM((LAYERS, 3 * D, D), BF),
    pltpu.VMEM((LAYERS, D, D), BF),
    pltpu.VMEM((LAYERS, FF, D), BF),
    pltpu.VMEM((LAYERS, D, FF), BF),
]
BACKWARD_SCRATCH = [
    pltpu.VMEM((LAYERS, D, 3 * D), BF),
    pltpu.VMEM((LAYERS, D, D), BF),
    pltpu.VMEM((LAYERS, D, FF), BF),
    pltpu.VMEM((LAYERS, FF, D), BF),
]
VECTOR_SCRATCH = [
    pltpu.VMEM((LAYERS, OWNERS, SHARD_ROWS, 128), F32),
    pltpu.VMEM((LAYERS, D, 128), F32),
    pltpu.VMEM((LAYERS, OWNERS, 4, 8, 128), F32),
]
TOTALS = ("qkv", "proj", "up", "down", "down_bias")
TOTAL_SCRATCH = [
    pltpu.VMEM((LAYERS, D + 16, 3 * D), F32),
    pltpu.VMEM((LAYERS, D + 16, D), F32),
    pltpu.VMEM((LAYERS, FF, 2 * D), F32),
    pltpu.VMEM((LAYERS, FF, D), F32),
    pltpu.VMEM((LAYERS, 8, D), F32),
]


def key_bias_rows(field_row, length):
    tokens = field_row.shape[1]
    at = lax.broadcasted_iota(jnp.int32, (1, tokens), 1)
    shut = jnp.where(field_row == 0, NEGATIVE, jnp.where(at >= length, NEGATIVE, 0.0))
    place = lax.broadcasted_iota(jnp.int32, (16, tokens), 0)
    rows = jnp.where(place == 0, jnp.broadcast_to(shut, (16, tokens)), 0.0)
    return jnp.concatenate([flip(rows), jnp.zeros((tokens, D - 16), F32)], axis=1).astype(BF)


def run_together(generators):
    results = [None] * len(generators)
    live = list(range(len(generators)))
    while live:
        for index in list(live):
            try:
                next(generators[index])
            except StopIteration as stop:
                results[index] = stop.value
                live.remove(index)
    return results


def layers_kernel(
    names, me_ref, length_ref, tokens_ref, field_ref, cot_ref, own_ref, other_ref, output_ref, grad_ref, send_ref, *scratch
):
    forward, backward, (stage, vec, up_bias) = scratch[:4], scratch[4:8], scratch[8:11]
    totals, kept = scratch[11:16], scratch[16:]
    seqs, tokens = field_ref.shape[0], field_ref.shape[2]
    me, core = me_ref[0], me_ref[1]
    unpack(me, own_ref, stage.at[core])
    unpack(me, other_ref, stage.at[1 - core])
    total = [dict(zip(TOTALS, [ref.at[layer] for ref in totals])) for layer in range(LAYERS)]
    for layer in range(LAYERS):
        unpack_forward(stage.at[layer], *[ref.at[layer] for ref in forward])
        unpack_backward(stage.at[layer], *[ref.at[layer] for ref in backward])
        unpack_vectors(stage.at[layer], vec.at[layer], up_bias.at[layer])
        for ref in total[layer].values():
            ref[...] = jnp.zeros_like(ref)

    def chain(seq, slot):
        at = pl.ds(seq * tokens, tokens)
        bias = key_bias_rows(field_ref[seq], length_ref[seq])
        state = flip(tokens_ref[at, :]).astype(F32)
        saved = [as_kept(names, [ref.at[slot, layer] for ref in kept]) for layer in range(LAYERS)]
        for layer in range(LAYERS):
            w = (*[ref.at[layer] for ref in forward], vec.at[layer], up_bias[layer].reshape(FF, 128))
            state = yield from layer_forward(state, bias, w, saved[layer])
        output_ref[at, :] = flip(state.astype(BF))
        grad_rows = cot_ref[at, :]
        grad = flip(grad_rows).astype(F32)
        for layer in reversed(range(LAYERS)):
            w = (*[ref.at[layer] for ref in backward], vec.at[layer])
            if layer < LAYERS - 1:
                grad_rows = flip(grad.astype(BF))
            grad = yield from layer_backward(grad, grad_rows, w, saved[layer], total[layer])
        grad_ref[at, :] = flip(grad)

    def together(seq_list):
        run_together([chain(seq, slot) for slot, seq in enumerate(seq_list)])

    pairs = (seqs - GROUP - seqs % GROUP) // GROUP if seqs % GROUP else seqs // GROUP
    pairs = max(pairs, 0)

    def pair(index, carry):
        together([index * GROUP + k for k in range(GROUP)])
        return carry

    lax.fori_loop(0, pairs, pair, 0)
    if pairs * GROUP < seqs:
        together(list(range(pairs * GROUP, seqs)))
    for layer in range(LAYERS):
        pack_grads(me, total[layer], send_ref.at[jnp.bitwise_xor(core, layer)])


def run_layers(place, lengths, tokens, fields, cotangent, own, other):
    seqs, _, length = fields.shape
    shapes = kept_shapes(length)
    slots = GROUP + seqs % GROUP if seqs > GROUP else seqs
    smem, vmem = pl.BlockSpec(memory_space=pltpu.SMEM), pl.BlockSpec(memory_space=pltpu.VMEM)
    return pl.pallas_call(
        functools.partial(layers_kernel, tuple(shapes)),
        in_specs=[smem, smem] + [vmem] * 5,
        out_specs=[vmem] * 3,
        out_shape=[
            jax.ShapeDtypeStruct(tokens.shape, BF),
            jax.ShapeDtypeStruct(tokens.shape, F32),
            jax.ShapeDtypeStruct((LAYERS, OWNERS, GRAD_ROWS, 128), BF),
        ],
        scratch_shapes=FORWARD_SCRATCH
        + BACKWARD_SCRATCH
        + VECTOR_SCRATCH
        + TOTAL_SCRATCH
        + [pltpu.VMEM((slots, LAYERS, *shape), dtype) for shape, dtype in shapes.values()],
        compiler_params=pltpu.CompilerParams(vmem_limit_bytes=VMEM_BYTES),
        name="layers",
    )(place, lengths, tokens, fields, cotangent, own, other)


def pack_kernel(me_ref, attn, qb, vb, proj, pb, ag, ash, up, ub, down, db, fg, fsh, shard_ref, own_ref):
    for layer in range(LAYERS):
        one = slice(layer, layer + 1)
        rows = [ref[one].astype(F32) for ref in (qb, vb, pb, ag, ash, db, fg, fsh)]
        bias = ub[one].astype(F32)
        rows += [bias[:, 8 * part : 8 * part + 8] for part in range(4)] + [jnp.zeros((4, 8), F32)]
        rows = jnp.concatenate(rows, axis=0)
        rows = jnp.concatenate([rows, jnp.zeros((16, 120), F32)], axis=1)
        small = flip(jnp.concatenate([rows, jnp.zeros((112, 128), F32)], axis=0))[:8]
        pieces = []
        for ref in (attn, proj, up):
            matrix = ref[layer].astype(F32)
            pieces += [matrix[:, 128 * part : 128 * (part + 1)] for part in range(matrix.shape[1] // 128)]
        shard_ref[layer] = jnp.concatenate(pieces + [down[layer].astype(F32), small], axis=0).astype(BF)
    own_ref[...] = shard_ref[me_ref[1]]


def run_pack(place, weights):
    vmem = pl.BlockSpec(memory_space=pltpu.VMEM)
    return pl.pallas_call(
        pack_kernel,
        in_specs=[pl.BlockSpec(memory_space=pltpu.SMEM)] + [vmem] * 13,
        out_specs=[vmem] * 2,
        out_shape=[
            jax.ShapeDtypeStruct((LAYERS, SHARD_ROWS, 128), BF),
            jax.ShapeDtypeStruct((SHARD_ROWS, 128), BF),
        ],
        name="pack",
    )(place, *weights)


def finish_kernel(me_ref, own_ref, other_ref, shard_ref, *outs):
    (attn, query_bias, value_bias, proj, proj_bias, attn_gain, attn_shift, up, up_bias, down, down_bias, ffn_gain, ffn_shift) = outs
    lane = lax.broadcasted_iota(jnp.int32, (8, 128), 1)
    for layer in range(LAYERS):
        red = jnp.where(me_ref[1] == layer, own_ref[...], other_ref[...])
        own = shard_ref[layer].astype(F32)
        small_in = own[96:104]
        small, whole = red[96:104], red[104:112]
        gains = [None, None]
        shifts = [None, None]
        for index, (places, gain_at, shift_at, target) in enumerate(
            (((0, 8, 16), ATTN_GAIN, ATTN_SHIFT, attn), ((32, 40, 48, 56), FFN_GAIN, FFN_SHIFT, up))
        ):
            gain, shift = small_in[:, gain_at : gain_at + 1], small_in[:, shift_at : shift_at + 1]
            first = 0 if index == 0 else 3
            gain_sum = jnp.zeros((8, 128), F32)
            shift_sum = jnp.zeros((8, 128), F32)
            for part, place in enumerate(places):
                grad, weight = red[place : place + 8], own[place : place + 8]
                column_sum = whole[first + part : first + part + 1]
                target[layer, :, 128 * part : 128 * (part + 1)] = gain * grad + shift * column_sum
                gain_sum += weight * grad
                shift_sum += weight * column_sum
            gains[index] = jnp.sum(gain_sum, axis=1, keepdims=True)
            shifts[index] = jnp.sum(shift_sum, axis=1, keepdims=True)
        proj[layer] = red[24:32]
        down[layer] = red[64:96]
        for at, column in ((8, gains[0]), (9, shifts[0]), (10, gains[1]), (11, shifts[1])):
            small = jnp.where(lane == at, jnp.broadcast_to(column, (8, 128)), small)
        rows = flip(small)
        query_bias[layer : layer + 1] = rows[0:1]
        value_bias[layer : layer + 1] = rows[1:2]
        proj_bias[layer : layer + 1] = rows[2:3]
        down_bias[layer : layer + 1] = rows[3:4]
        up_bias[layer : layer + 1] = jnp.concatenate([rows[4 + part : 5 + part] for part in range(4)], axis=1)
        attn_gain[layer : layer + 1] = rows[8:9]
        attn_shift[layer : layer + 1] = rows[9:10]
        ffn_gain[layer : layer + 1] = rows[10:11]
        ffn_shift[layer : layer + 1] = rows[11:12]


def run_finish(place, own, other, shard):
    layers = LAYERS
    vector = jax.ShapeDtypeStruct((layers, 8), F32)

    def matrix(rows, columns):
        return jax.ShapeDtypeStruct((layers, rows, columns), F32)

    shapes = [
        matrix(8, 3 * D), vector, vector, matrix(8, D), vector, vector, vector, matrix(8, FF),
        jax.ShapeDtypeStruct((layers, 32), F32), matrix(32, D), vector, vector, vector,
    ]
    return pl.pallas_call(
        finish_kernel,
        in_specs=[pl.BlockSpec(memory_space=pltpu.SMEM)] + [pl.BlockSpec(memory_space=pltpu.VMEM)] * 3,
        out_specs=[pl.BlockSpec(memory_space=pltpu.VMEM)] * len(shapes),
        out_shape=shapes,
        name="finish",
    )(place, own, other, shard)


def pack_weights(weights, layer, owners):
    attn, qb, vb, proj, pb, ag, ash, up, ub, down, db, fg, fsh = (w[layer] for w in weights)

    def blocks(matrix, count):
        return [matrix[:, 128 * part : 128 * (part + 1)].reshape(owners, 8, 128) for part in range(count)]

    vectors = [v.reshape(owners, 8, 1) for v in (qb, vb, pb, ag, ash, db, fg, fsh)]
    bias = jnp.swapaxes(ub.reshape(owners, 4, 8), 1, 2)
    small = jnp.concatenate(vectors + [bias], axis=2)
    small = jnp.pad(small, ((0, 0), (0, 0), (0, 128 - small.shape[2])))
    return jnp.concatenate(
        blocks(attn, 3) + blocks(proj, 1) + blocks(up, 4) + [down.reshape(owners, 32, 128), small], axis=1
    )


def exchange(x, bit):
    return lax.ppermute(x, "wide", [(i, i ^ bit) for i in range(OWNERS)])


def swap_cores(x):
    return lax.ppermute(x, "dp", [(0, 1), (1, 0)])


def gather_doubling(own):
    held = own[None]
    for bit in (8, 4, 2, 1):
        held = jnp.concatenate([held, exchange(held, bit)], axis=0)
    return held


def reduce_halving(send):
    held = send[0].astype(F32) + swap_cores(send[1]).astype(F32)
    for bit in (1, 2, 4, 8):
        half = held.shape[0] // 2
        keep, away = held[:half], held[half:]
        held = keep + exchange(away.astype(BF), bit).astype(F32)
    return held[0]


def reduce_general(send, weights, gathered, layer):
    order = [reverse_bits(owner) for owner in range(OWNERS)]
    total = jnp.stack([send[place] for place in order]).astype(F32)

    def matrix(places):
        return jnp.concatenate([total[:, p : p + 8].reshape(D, 128) for p in places], axis=1)

    attn, up, proj = matrix((0, 8, 16)), matrix((32, 40, 48, 56)), matrix((24,))
    down = total[:, 64:96].reshape(FF, D)
    small, whole = total[:, 96:104].reshape(D, 128), total[0, 104:112]
    attn_w, up_w = gathered[0][layer].astype(F32), gathered[7][layer].astype(F32)
    again, ashift, fgain, fshift = (gathered[i][layer].astype(F32)[:, None] for i in (5, 6, 11, 12))
    attn_sum, up_sum = whole[0:3].reshape(1, 3 * D), whole[3:7].reshape(1, FF)
    up_bias = jnp.swapaxes(total[:, 96:104, 4:8], 1, 2).reshape(FF)
    local = (
        again * attn + ashift * attn_sum, small[:, 0], small[:, 1], proj, small[:, 2],
        jnp.sum(attn_w * attn, axis=1), jnp.sum(attn_w * attn_sum, axis=1),
        fgain * up + fshift * up_sum, up_bias, down, small[:, 3],
        jnp.sum(up_w * up, axis=1), jnp.sum(up_w * up_sum, axis=1),
    )
    return tuple(
        lax.psum_scatter(lax.psum(g, "dp"), "wide", scatter_dimension=0, tiled=True) for g in local
    )


def body(tokens, field_ids, seq_lengths, cotangent, *weights, owners):
    seqs = seq_lengths.shape[0]
    fields = field_ids.reshape(seqs, 1, -1)
    doubling = owners == OWNERS
    if doubling:
        place = jnp.stack([lax.axis_index("wide"), lax.axis_index("dp")]).astype(jnp.int32)
        shard, own = run_pack(place, weights)
        own = gather_doubling(own)
        other = swap_cores(own)
    else:
        place = jnp.zeros((2,), jnp.int32)
        gathered = [lax.all_gather(w, "wide", axis=1, tiled=True) for w in weights]
        order = [reverse_bits(owner) for owner in range(OWNERS)]
        packed = [pack_weights(gathered, layer, OWNERS) for layer in range(LAYERS)]
        own, other = (jnp.stack([p[owner] for owner in order]) for p in packed)
    output, token_grad, send = run_layers(place, seq_lengths, tokens, fields, cotangent, own, other)
    if doubling:
        reduced = reduce_halving(send)
        grads = run_finish(place, reduced, swap_cores(reduced), shard)
    else:
        by_layer = [reduce_general(send[layer], weights, gathered, layer) for layer in range(LAYERS)]
        grads = [jnp.stack(pair) for pair in zip(*by_layer)]
    return (output, token_grad, *grads)


def solution(mesh):
    rows, vector = P(("dp", "wide"), None), P(("dp", "wide"))
    flat, square = P(None, "wide"), P(None, "wide", None)
    params = (square, flat, flat, square, flat, flat, flat, square, flat, square, flat, flat, flat)
    return jax.shard_map(
        functools.partial(body, owners=mesh.shape["wide"]),
        mesh=mesh,
        in_specs=(rows, vector, vector, rows, *params),
        out_specs=(rows, rows, *params),
        check_vma=False,
    )
```

```python
import functools
import math

import jax
import jax.numpy as jnp
from jax import lax
from jax.experimental import pallas as pl
from jax.experimental.pallas import tpu as pltpu
from jax.sharding import PartitionSpec as P

HEADS = 4
EPSILON = 1e-05
NEGATIVE = -1e30
BLOCK = 128
D = 128
FF = 512
OWNERS = 16
SHARD_ROWS = 104
GRAD_ROWS = 112
LAYERS = 2
GROUP = 2
SPAN = 256
CHUNK = 256
VMEM_BYTES = 54 * 2**20

BF = jnp.bfloat16
F32 = jnp.float32
NN = (((1,), (0,)), ((), ()))


def dot(a, b):
    return lax.dot_general(a, b, NN, preferred_element_type=F32)


def flip(x):
    return jnp.transpose(x)


def col(vec_ref, index):
    return vec_ref[:, index : index + 1]


STEP_BITS = ((8, 4, 2, 1), (4, 8, 1, 2))


def place_of(relative, core):
    first = ((relative & 1) << 3) | ((relative & 2) << 1) | ((relative & 4) >> 1) | ((relative & 8) >> 3)
    return first if core == 0 else ((first & 5) << 1) | ((first & 10) >> 1)


def place_by(relative, core):
    return jnp.where(core == 0, place_of(relative, 0), place_of(relative, 1))


def position(known):
    return (lax.axis_index("wide"), lax.axis_index("dp")) if known else (jnp.int32(0), jnp.int32(0))


def unpack(me, core, packed_ref, stage):
    for owner in range(OWNERS):
        stage[owner] = packed_ref[place_by(jnp.bitwise_xor(me, owner), core)].astype(F32)


def stage_rows(stage, start, count):
    return stage[:, start : start + count, :].reshape(OWNERS * count, 128)


def unpack_forward(stage, qkv_t, proj_t, up_t, down_t):
    for part in range(3):
        qkv_t[part * D : (part + 1) * D, :] = flip(stage_rows(stage, 8 * part, 8)).astype(BF)
    proj_t[...] = flip(stage_rows(stage, 24, 8)).astype(BF)
    for part in range(4):
        up_t[part * D : (part + 1) * D, :] = flip(stage_rows(stage, 32 + 8 * part, 8)).astype(BF)
    down_t[...] = flip(stage_rows(stage, 64, 32)).astype(BF)


def unpack_backward(stage, qkv, proj, up, down):
    for part in range(3):
        qkv[:, part * D : (part + 1) * D] = stage_rows(stage, 8 * part, 8).astype(BF)
    proj[...] = stage_rows(stage, 24, 8).astype(BF)
    for part in range(4):
        up[:, part * D : (part + 1) * D] = stage_rows(stage, 32 + 8 * part, 8).astype(BF)
    down[...] = stage_rows(stage, 64, 32).astype(BF)


def unpack_vectors(stage, vec, up_bias):
    small = stage[:, 96:104, :]
    vec[...] = small.reshape(D, 128)
    for part in range(4):
        piece = small[:, :, 8 + part : 9 + part]
        up_bias[:, part, :, :] = jnp.broadcast_to(piece, (OWNERS, 8, 128))


QUERY_BIAS, VALUE_BIAS, PROJ_BIAS, ATTN_GAIN, ATTN_SHIFT, DOWN_BIAS, FFN_GAIN, FFN_SHIFT = range(8)


def norm_stats(x):
    mean = jnp.mean(x, axis=0, keepdims=True)
    centred = x - mean
    spread = jnp.mean(centred * centred, axis=0, keepdims=True)
    rstd = lax.rsqrt(spread + EPSILON)
    return centred * rstd, rstd


def norm_backward(grad_out, gain, unit, rstd):
    weighted = grad_out * gain
    first = jnp.mean(weighted, axis=0, keepdims=True)
    second = jnp.mean(weighted * unit, axis=0, keepdims=True)
    return rstd * (weighted - first - unit * second)


def head_columns(x, block, heads):
    size = D // HEADS
    piece = x[:, block * BLOCK : (block + 1) * BLOCK]
    columns = []
    for head in heads:
        rows = [
            piece[head * size : (head + 1) * size] if other == head else jnp.zeros((size, BLOCK), piece.dtype)
            for other in range(HEADS)
        ]
        columns.append(jnp.concatenate(rows, axis=0))
    return jnp.concatenate(columns, axis=1)


def head_rows(x, block, heads):
    size = D // HEADS
    piece = x[block * BLOCK : (block + 1) * BLOCK, :]
    lane = lax.broadcasted_iota(jnp.int32, (BLOCK, D), 1) // size
    return jnp.concatenate([jnp.where(lane == head, piece, jnp.zeros_like(piece)) for head in heads], axis=0)


def own_columns(x, heads):
    size = D // HEADS
    return jnp.concatenate(
        [x[head * size : (head + 1) * size, at * BLOCK : (at + 1) * BLOCK] for at, head in enumerate(heads)], axis=0
    )


def head_spread(rows):
    size = D // HEADS
    return jnp.concatenate(
        [jnp.broadcast_to(rows[head : head + 1], (size, rows.shape[1])) for head in range(HEADS)], axis=0
    )


def extra_rows(rows, total=D):
    width = rows[0].shape[1]
    filled = jnp.zeros((16, width), F32)
    place = lax.broadcasted_iota(jnp.int32, (16, width), 0)
    for index, row in enumerate(rows):
        filled = jnp.where(place == index, jnp.broadcast_to(row, (16, width)), filled)
    return jnp.concatenate([filled.astype(BF), jnp.zeros((total - 16, width), BF)], axis=0)


PAIRS = ((0, 1, 2, 3),)


def attend_forward(x, key_bias, own_bias, w, save):
    qkv_t, _, _, _, vec, _ = w
    tokens = x.shape[1]
    blocks = tokens // BLOCK
    size = D // HEADS
    unit, rstd = norm_stats(x)
    normed = (unit * col(vec, ATTN_GAIN) + col(vec, ATTN_SHIFT)).astype(BF)
    save["unit"][...] = unit.astype(BF)
    save["rows"][0:1] = rstd
    yield
    factor = size ** (-0.5) / math.log(2.0)
    query = ((dot(qkv_t[:D], normed) + col(vec, QUERY_BIAS)) * factor).astype(BF)
    save["query"][...] = query
    yield
    key = dot(qkv_t[D : 2 * D], normed).astype(BF)
    save["key"][...] = key
    key_plain = flip(key)
    key_rows = jnp.concatenate([key_plain, key_bias], axis=1)
    yield
    value = (dot(qkv_t[2 * D :], normed) + col(vec, VALUE_BIAS)).astype(BF)
    save["value"][...] = value
    value_ones = jnp.concatenate([value, jnp.ones((16, tokens), BF)], axis=0)
    ones = extra_rows([jnp.ones((1, len(PAIRS[0]) * BLOCK), F32)])
    for block in range(blocks):
        seen = (block + 1) * BLOCK
        at = slice(block * BLOCK, seen)
        for pair, heads in enumerate(PAIRS):
            yield
            columns = head_columns(query, block, heads)
            scores = dot(key_plain[seen - BLOCK : seen], columns) + jnp.concatenate([own_bias[block]] * len(heads), axis=1)
            if block:
                right = jnp.concatenate([columns, ones], axis=0)
                scores = jnp.concatenate([dot(key_rows[: seen - BLOCK], right), scores], axis=0)
            raised = jnp.exp2(scores - jnp.max(scores, axis=0, keepdims=True)).astype(BF)
            save["probs"][block][:, pair * len(heads) * BLOCK : (pair + 1) * len(heads) * BLOCK] = raised
            yield
            summed = dot(value_ones[:, :seen], raised)
            total = summed[D : D + 1]
            inv = 1.0 / total
            for place, head in enumerate(heads):
                save["rows"][2 + head : 3 + head, at] = inv[:, place * BLOCK : (place + 1) * BLOCK]
            save["attended"][heads[0] * size : (heads[-1] + 1) * size, at] = own_columns(summed[:D] * inv, heads)


def feed_forward(x, w, save):
    _, proj_t, up_t, down_t, vec, up_bias = w
    tokens = x.shape[1]
    middle = x + (dot(proj_t[...], save["attended"][...].astype(BF)) + col(vec, PROJ_BIAS))
    yield
    unit_two, rstd_two = norm_stats(middle)
    save["unit_two"][...] = unit_two.astype(BF)
    save["rows"][1:2] = rstd_two
    normed_two = (unit_two * col(vec, FFN_GAIN) + col(vec, FFN_SHIFT)).astype(BF)
    root = math.sqrt(2.0 / math.pi)
    result = []
    for start in range(0, tokens, SPAN):
        at = slice(start, start + SPAN)
        for row in range(0, FF, CHUNK):
            yield
            rows = slice(row, row + CHUNK)
            bias = jnp.concatenate([up_bias[rows]] * (SPAN // 128), axis=1)
            expanded = dot(up_t[rows], normed_two[:, at]) + bias
            square = expanded * expanded
            bent = jnp.tanh(expanded * (root + (root * 0.044715) * square))
            half = 0.5 + 0.5 * bent
            active = expanded * half
            save["active"][rows, at] = active.astype(BF)
            slope = half + active * ((1.0 - bent) * (root + (3.0 * root * 0.044715) * square))
            save["slope"][rows, at] = slope.astype(BF)
        yield
        result.append(middle[:, at] + col(vec, DOWN_BIAS) + dot(down_t[...], save["active"][:, at]))
    return jnp.concatenate(result, axis=1)


def feed_backward(grad, grad_rows, w, kept, total):
    _, _, up, down, vec = w
    tokens = grad.shape[1]
    grad_low = grad.astype(BF)
    for start in range(0, tokens, SPAN):
        at = slice(start, start + SPAN)
        for row in range(0, FF, CHUNK):
            rows = slice(row, row + CHUNK)
            grad_active = dot(down[rows], grad_low[:, at])
            kept["grad_exp"][rows, at] = (grad_active * kept["slope"][rows, at].astype(F32)).astype(BF)
            yield
    unit_two = kept["unit_two"][...]
    normed = dot(up[...], kept["grad_exp"][...])
    yield
    lane = lax.broadcasted_iota(jnp.int32, (tokens, D), 1)
    ones_lane = jnp.where(lane == 0, 1.0, 0.0).astype(BF)
    unit_two_rows = jnp.concatenate([flip(unit_two), ones_lane], axis=1)
    for row in range(0, FF, CHUNK):
        rows = slice(row, row + CHUNK)
        total["down"][rows] += dot(kept["active"][rows], grad_rows)
        yield
        total["up"][rows] += dot(kept["grad_exp"][rows], unit_two_rows)
        yield
    total["down_bias"][...] += dot(jnp.ones((16, tokens), BF), grad_rows)[:8]
    return grad + norm_backward(normed, col(vec, FFN_GAIN), unit_two.astype(F32), kept["rows"][1:2])


def attend_backward(grad_middle, w, kept, total):
    qkv, proj, _, _, vec = w
    tokens = grad_middle.shape[1]
    blocks = tokens // BLOCK
    size = D // HEADS
    ones_row = jnp.ones((16, tokens), BF)
    lane = lax.broadcasted_iota(jnp.int32, (tokens, D), 1)
    grad_proj = grad_middle.astype(BF)
    attended = kept["attended"][...]
    total["proj"][...] += dot(jnp.concatenate([attended.astype(BF), ones_row], axis=0), flip(grad_proj))
    yield
    grad_attended = dot(proj[...], grad_proj).astype(BF).astype(F32)
    scaled = (grad_attended * head_spread(kept["rows"][2 : 2 + HEADS])).astype(BF)
    yield
    product = scaled.astype(F32) * attended
    centre = [jnp.sum(product[h * size : (h + 1) * size], axis=0, keepdims=True) for h in range(HEADS)]
    centre_high = [c.astype(BF).astype(F32) for c in centre]
    centre_low = [c - high for c, high in zip(centre, centre_high)]
    minus = jnp.where(lane < 2, -1.0, 0.0).astype(BF)
    value_rows = jnp.concatenate([flip(kept["value"][...]), minus], axis=1)
    key = kept["key"][...]
    query_rows = flip(kept["query"][...])
    scaled_rows = flip(scaled)
    grad_query = []
    grad_value = [None] * blocks
    grad_key = [None] * blocks

    def gather_row(parts, block, heads):
        return jnp.concatenate([parts[h][:, block * BLOCK : (block + 1) * BLOCK] for h in heads], axis=1)

    for block in range(blocks):
        seen = (block + 1) * BLOCK
        for pair, heads in enumerate(PAIRS):
            yield
            right = jnp.concatenate(
                [
                    head_columns(scaled, block, heads),
                    extra_rows([gather_row(centre_high, block, heads), gather_row(centre_low, block, heads)]),
                ],
                axis=0,
            )
            grad_probs = dot(value_rows[:seen], right)
            raised = kept["probs"][block][:, pair * len(heads) * BLOCK : (pair + 1) * len(heads) * BLOCK]
            grad_scores = raised * grad_probs.astype(BF)
            yield
            grad_query.append(own_columns(dot(key[:, :seen], grad_scores), heads))
            yield
            value_part = dot(raised, head_rows(scaled_rows, block, heads))
            for j in range(block + 1):
                v = value_part[j * BLOCK : (j + 1) * BLOCK]
                grad_value[j] = v if grad_value[j] is None else grad_value[j] + v
            yield
            key_part = dot(grad_scores, head_rows(query_rows, block, heads))
            for j in range(block + 1):
                k = key_part[j * BLOCK : (j + 1) * BLOCK]
                grad_key[j] = k if grad_key[j] is None else grad_key[j] + k
    yield
    grad_query = [jnp.concatenate(grad_query[len(PAIRS) * block : len(PAIRS) * (block + 1)], axis=0) for block in range(blocks)]
    grad_query = (jnp.concatenate(grad_query, axis=1) * size ** (-0.5)).astype(BF)
    grad_key = (jnp.concatenate(grad_key, axis=0) * math.log(2.0)).astype(BF)
    grad_value = jnp.concatenate(grad_value, axis=0).astype(BF)
    packed_rows = jnp.concatenate([flip(grad_query), grad_key, grad_value], axis=1)
    packed = jnp.concatenate([grad_query, flip(grad_key), flip(grad_value)], axis=0)
    yield
    unit = kept["unit"][...]
    total["qkv"][...] += dot(jnp.concatenate([unit, ones_row], axis=0), packed_rows)
    yield
    grad_normed = dot(qkv[...], packed)
    return grad_middle + norm_backward(grad_normed, col(vec, ATTN_GAIN), unit.astype(F32), kept["rows"][0:1])


def pack_grads(me, core, total, send):
    qkv, proj, up, down, down_bias = (total[n] for n in ("qkv", "proj", "up", "down", "down_bias"))
    up_t = [flip(up[D * part : D * (part + 1), :D]) for part in range(4)]
    up_sum = up[:, D:]
    up_sum_rows = [flip(up_sum[D * part : D * (part + 1)])[0:1] for part in range(4)]
    sums = jnp.concatenate(
        [
            qkv[D : D + 1, :D],
            qkv[D : D + 1, 2 * D : 3 * D],
            proj[D : D + 1],
            down_bias[0:1],
            jnp.zeros((D - 4, D), F32),
        ],
        axis=0,
    )
    columns = flip(sums)
    lane = lax.broadcasted_iota(jnp.int32, (8, 128), 1)
    whole = jnp.concatenate(
        [qkv[D : D + 1, D * part : D * (part + 1)] for part in range(3)]
        + up_sum_rows
        + [jnp.zeros((1, D), F32)],
        axis=0,
    )
    for owner in range(OWNERS):
        own = slice(8 * owner, 8 * owner + 8)
        small = jnp.where(lane < 4, columns[own], 0.0)
        for part in range(4):
            at = 32 * owner + 8 * part
            small = jnp.where(lane == 4 + part, jnp.broadcast_to(up_sum[at : at + 8, 0:1], (8, 128)), small)
        pieces = (
            [qkv[own, D * part : D * (part + 1)] for part in range(3)]
            + [proj[own]]
            + [u[own] for u in up_t]
            + [down[32 * owner : 32 * owner + 32], small, whole]
        )
        send[place_by(jnp.bitwise_xor(me, owner), core)] = jnp.concatenate(pieces, axis=0).astype(BF)


KEPT = ("unit", "query", "key", "value", "attended", "unit_two", "rows", "active", "slope")


def kept_shapes(tokens):
    shapes = {name: ((D, tokens), BF) for name in KEPT}
    shapes["rows"] = ((8, tokens), F32)
    shapes["attended"] = ((D, tokens), F32)
    shapes["active"] = ((FF, tokens), BF)
    shapes["slope"] = ((FF, tokens), BF)
    shapes["grad_exp"] = ((FF, tokens), BF)
    for block in range(tokens // BLOCK):
        shapes[f"probs{block}"] = (((block + 1) * BLOCK, HEADS * BLOCK), BF)
    return shapes


def as_kept(names, refs):
    kept = dict(zip(names, refs))
    probs = [kept.pop(n) for n in names if n.startswith("probs")]
    kept["probs"] = probs
    return kept


FORWARD_SCRATCH = [
    pltpu.VMEM((LAYERS, 3 * D, D), BF),
    pltpu.VMEM((LAYERS, D, D), BF),
    pltpu.VMEM((LAYERS, FF, D), BF),
    pltpu.VMEM((LAYERS, D, FF), BF),
]
BACKWARD_SCRATCH = [
    pltpu.VMEM((LAYERS, D, 3 * D), BF),
    pltpu.VMEM((LAYERS, D, D), BF),
    pltpu.VMEM((LAYERS, D, FF), BF),
    pltpu.VMEM((LAYERS, FF, D), BF),
]
VECTOR_SCRATCH = [
    pltpu.VMEM((LAYERS, OWNERS, SHARD_ROWS, 128), F32),
    pltpu.VMEM((LAYERS, D, 128), F32),
    pltpu.VMEM((LAYERS, OWNERS, 4, 8, 128), F32),
]
TOTALS = ("qkv", "proj", "up", "down", "down_bias")
TOTAL_SCRATCH = [
    pltpu.VMEM((LAYERS, D + 16, 3 * D), F32),
    pltpu.VMEM((LAYERS, D + 16, D), F32),
    pltpu.VMEM((LAYERS, FF, 2 * D), F32),
    pltpu.VMEM((LAYERS, FF, D), F32),
    pltpu.VMEM((LAYERS, 8, D), F32),
]


def key_bias_rows(field_row, length):
    tokens = field_row.shape[1]
    at = lax.broadcasted_iota(jnp.int32, (1, tokens), 1)
    shut = jnp.where(field_row == 0, NEGATIVE, jnp.where(at >= length, NEGATIVE, 0.0))
    place = lax.broadcasted_iota(jnp.int32, (16, tokens), 0)
    rows = jnp.where(place == 0, jnp.broadcast_to(shut, (16, tokens)), 0.0)
    columns = flip(rows)
    low = jnp.concatenate([columns, jnp.zeros((tokens, D - 16), F32)], axis=1).astype(BF)
    key_at = lax.broadcasted_iota(jnp.int32, (BLOCK, BLOCK), 0)
    query_at = lax.broadcasted_iota(jnp.int32, (BLOCK, BLOCK), 1)
    own = []
    for block in range(tokens // BLOCK):
        column = jnp.broadcast_to(columns[block * BLOCK : (block + 1) * BLOCK, 0:1], (BLOCK, BLOCK))
        own.append(jnp.where(key_at < query_at, column, jnp.where(key_at == query_at, 0.0, NEGATIVE)))
    return low, own


FORWARD_STEPS = (12, 8)
BACKWARD_STEPS = (10, 21)


def run_together(chains):
    results = [None] * len(chains)
    done = [0.0] * len(chains)
    rate = [[1.0 / steps for layer in range(LAYERS) for steps in phases for _ in range(steps)] for _, phases in chains]
    count = [0] * len(chains)
    live = list(range(len(chains)))
    while live:
        index = min(live, key=lambda i: done[i])
        try:
            next(chains[index][0])
            done[index] += rate[index][min(count[index], len(rate[index]) - 1)]
            count[index] += 1
        except StopIteration as stop:
            results[index] = stop.value
            live.remove(index)
    return results


def layers_kernel(
    names, known, length_ref, tokens_ref, field_ref, cot_ref, own_ref, other_ref, output_ref, grad_ref, keep_ref, away_ref, *scratch
):
    forward, backward, (stage, vec, up_bias) = scratch[:4], scratch[4:8], scratch[8:11]
    totals, kept = scratch[11:16], scratch[16:]
    seqs, tokens = field_ref.shape[0], field_ref.shape[2]
    me, core = position(known)
    unpack(me, core, own_ref, stage.at[core])
    unpack(me, 1 - core, other_ref, stage.at[1 - core])

    def total_of(layer):
        return dict(zip(TOTALS, [ref.at[layer] for ref in totals]))

    total = [total_of(layer) for layer in range(LAYERS)]
    for layer in range(LAYERS):
        unpack_forward(stage.at[layer], *[ref.at[layer] for ref in forward])
        unpack_backward(stage.at[layer], *[ref.at[layer] for ref in backward])
        unpack_vectors(stage.at[layer], vec.at[layer], up_bias.at[layer])

    def clear():
        for ref in totals:
            ref[...] = jnp.zeros_like(ref)

    def saved(slot, layer):
        n=len(names)
        return as_kept(names, [ref.at[layer] for ref in kept[slot*n:(slot+1)*n]])

    def rows_of(seq):
        return pl.ds(pl.multiple_of(seq * tokens, tokens), tokens)

    def forward_chain(seq, slot):
        bias, own_bias = key_bias_rows(field_ref[seq], length_ref[seq])
        state = flip(tokens_ref[rows_of(seq), :]).astype(F32)
        for layer in range(LAYERS):
            w = (*[ref.at[layer] for ref in forward], vec.at[layer], up_bias[layer].reshape(FF, 128))
            save = saved(slot, layer)
            yield from attend_forward(state, bias, own_bias, w, save)
            yield
            state = yield from feed_forward(state, w, save)
            yield
        output_ref[rows_of(seq), :] = flip(state.astype(BF))

    def backward_chain(seq, slot):
        grad_rows = cot_ref[rows_of(seq), :]
        grad = flip(grad_rows).astype(F32)
        for layer in reversed(range(LAYERS)):
            w = (*[ref.at[layer] for ref in backward], vec.at[layer])
            save = saved(slot, layer)
            if layer < LAYERS - 1:
                grad_rows = flip(grad.astype(BF))
            grad = yield from feed_backward(grad, grad_rows, w, save, total[layer])
            yield
            grad = yield from attend_backward(grad, w, save, total[layer])
            yield
        grad_ref[rows_of(seq), :] = flip(grad)

    def together(seq_list):
        run_together([(forward_chain(seq, slot), FORWARD_STEPS) for slot, seq in enumerate(seq_list)])
        run_together([(backward_chain(seq, slot), BACKWARD_STEPS) for slot, seq in enumerate(seq_list)])

    groups = seqs // GROUP if seqs % GROUP == 0 else max(seqs // GROUP - 1, 0)
    clear()

    def turn(index, carry):
        together([index * GROUP + k for k in range(GROUP)])
        return carry

    lax.fori_loop(0, groups, turn, 0)
    if groups * GROUP < seqs:
        rest = seqs - groups * GROUP

        def last(index, carry):
            together([groups * GROUP + index * rest + k for k in range(rest)])
            return carry

        lax.fori_loop(0, 1, last, 0)

    pack_grads(me, core, total_of(core), keep_ref)
    pack_grads(me, 1 - core, total_of(1 - core), away_ref)


def near(x):
    return pltpu.with_memory_space_constraint(x, pltpu.VMEM)


def run_layers(lengths, tokens, fields, cotangent, own, other, known):
    seqs, _, length = fields.shape
    shapes = kept_shapes(length)
    slots = min(seqs, GROUP + seqs % GROUP)
    smem, vmem = pl.BlockSpec(memory_space=pltpu.SMEM), pl.BlockSpec(memory_space=pltpu.VMEM)
    send = pltpu.VMEM((OWNERS, GRAD_ROWS, 128), BF)
    own, other = near(own), near(other)
    return pl.pallas_call(
        functools.partial(layers_kernel, tuple(shapes), known),
        in_specs=[smem] + [vmem] * 5,
        out_specs=[vmem] * 4,
        out_shape=[
            jax.ShapeDtypeStruct(tokens.shape, BF),
            jax.ShapeDtypeStruct(tokens.shape, F32),
            send,
            send,
        ],
        scratch_shapes=FORWARD_SCRATCH
        + BACKWARD_SCRATCH
        + VECTOR_SCRATCH
        + TOTAL_SCRATCH
        + [pltpu.VMEM((LAYERS, *shape), dtype) for _ in range(slots) for shape, dtype in shapes.values()],
        compiler_params=pltpu.CompilerParams(vmem_limit_bytes=VMEM_BYTES),
        name="layers",
    )(lengths, tokens, fields, cotangent, own, other)


def pack_kernel(attn, qb, vb, proj, pb, ag, ash, up, ub, down, db, fg, fsh, shard_ref, own_ref):
    for layer in range(LAYERS):
        one = slice(layer, layer + 1)
        rows = [ref[one].astype(F32) for ref in (qb, vb, pb, ag, ash, db, fg, fsh)]
        bias = ub[one].astype(F32)
        rows += [bias[:, 8 * part : 8 * part + 8] for part in range(4)] + [jnp.zeros((4, 8), F32)]
        rows = jnp.concatenate(rows, axis=0)
        rows = jnp.concatenate([rows, jnp.zeros((16, 120), F32)], axis=1)
        small = flip(jnp.concatenate([rows, jnp.zeros((112, 128), F32)], axis=0))[:8]
        pieces = []
        for ref in (attn, proj, up):
            matrix = ref[layer].astype(F32)
            pieces += [matrix[:, 128 * part : 128 * (part + 1)] for part in range(matrix.shape[1] // 128)]
        shard_ref[layer] = jnp.concatenate(pieces + [down[layer].astype(F32), small], axis=0).astype(BF)
    own_ref[0] = shard_ref[lax.axis_index("dp")]


def run_pack(weights):
    vmem = pl.BlockSpec(memory_space=pltpu.VMEM)
    return pl.pallas_call(
        pack_kernel,
        in_specs=[vmem] * 13,
        out_specs=[vmem] * 2,
        out_shape=[
            jax.ShapeDtypeStruct((LAYERS, SHARD_ROWS, 128), BF),
            pltpu.VMEM((1, SHARD_ROWS, 128), BF),
        ],
        name="pack",
    )(*weights)


def finish_kernel(own_ref, other_ref, shard_ref, *outs):
    (attn, query_bias, value_bias, proj, proj_bias, attn_gain, attn_shift, up, up_bias, down, down_bias, ffn_gain, ffn_shift) = outs
    lane = lax.broadcasted_iota(jnp.int32, (8, 128), 1)
    for layer in range(LAYERS):
        red = jnp.where(lax.axis_index("dp") == layer, own_ref[...], other_ref[...])
        own = shard_ref[layer].astype(F32)
        small_in = own[96:104]
        small, whole = red[96:104], red[104:112]
        gains = [None, None]
        shifts = [None, None]
        for index, (places, gain_at, shift_at, target) in enumerate(
            (((0, 8, 16), ATTN_GAIN, ATTN_SHIFT, attn), ((32, 40, 48, 56), FFN_GAIN, FFN_SHIFT, up))
        ):
            gain, shift = small_in[:, gain_at : gain_at + 1], small_in[:, shift_at : shift_at + 1]
            first = 0 if index == 0 else 3
            gain_sum = jnp.zeros((8, 128), F32)
            shift_sum = jnp.zeros((8, 128), F32)
            for part, place in enumerate(places):
                grad, weight = red[place : place + 8], own[place : place + 8]
                column_sum = whole[first + part : first + part + 1]
                target[layer, :, 128 * part : 128 * (part + 1)] = gain * grad + shift * column_sum
                gain_sum += weight * grad
                shift_sum += weight * column_sum
            gains[index] = jnp.sum(gain_sum, axis=1, keepdims=True)
            shifts[index] = jnp.sum(shift_sum, axis=1, keepdims=True)
        proj[layer] = red[24:32]
        down[layer] = red[64:96]
        for at, column in ((8, gains[0]), (9, shifts[0]), (10, gains[1]), (11, shifts[1])):
            small = jnp.where(lane == at, jnp.broadcast_to(column, (8, 128)), small)
        rows = flip(small)
        query_bias[layer : layer + 1] = rows[0:1]
        value_bias[layer : layer + 1] = rows[1:2]
        proj_bias[layer : layer + 1] = rows[2:3]
        down_bias[layer : layer + 1] = rows[3:4]
        up_bias[layer : layer + 1] = jnp.concatenate([rows[4 + part : 5 + part] for part in range(4)], axis=1)
        attn_gain[layer : layer + 1] = rows[8:9]
        attn_shift[layer : layer + 1] = rows[9:10]
        ffn_gain[layer : layer + 1] = rows[10:11]
        ffn_shift[layer : layer + 1] = rows[11:12]


def run_finish(own, other, shard):
    layers = LAYERS
    vector = jax.ShapeDtypeStruct((layers, 8), F32)

    def matrix(rows, columns):
        return jax.ShapeDtypeStruct((layers, rows, columns), F32)

    shapes = [
        matrix(8, 3 * D), vector, vector, matrix(8, D), vector, vector, vector, matrix(8, FF),
        jax.ShapeDtypeStruct((layers, 32), F32), matrix(32, D), vector, vector, vector,
    ]
    return pl.pallas_call(
        finish_kernel,
        in_specs=[pl.BlockSpec(memory_space=pltpu.VMEM)] * 3,
        out_specs=[pl.BlockSpec(memory_space=pltpu.VMEM)] * len(shapes),
        out_shape=shapes,
        name="finish",
    )(near(own), near(other), shard)


def pack_weights(weights, layer, owners):
    attn, qb, vb, proj, pb, ag, ash, up, ub, down, db, fg, fsh = (w[layer] for w in weights)

    def blocks(matrix, count):
        return [matrix[:, 128 * part : 128 * (part + 1)].reshape(owners, 8, 128) for part in range(count)]

    vectors = [v.reshape(owners, 8, 1) for v in (qb, vb, pb, ag, ash, db, fg, fsh)]
    bias = jnp.swapaxes(ub.reshape(owners, 4, 8), 1, 2)
    small = jnp.concatenate(vectors + [bias], axis=2)
    small = jnp.pad(small, ((0, 0), (0, 0), (0, 128 - small.shape[2])))
    return jnp.concatenate(
        blocks(attn, 3) + blocks(proj, 1) + blocks(up, 4) + [down.reshape(owners, 32, 128), small], axis=1
    )


def exchange(x, step):
    pairs = [
        (core * OWNERS + i, core * OWNERS + (i ^ bits[step])) for core, bits in enumerate(STEP_BITS) for i in range(OWNERS)
    ]
    return lax.ppermute(x, ("dp", "wide"), pairs)


def swap_cores(x):
    return lax.ppermute(x, "dp", [(0, 1), (1, 0)])


def gather_doubling(own):
    held = jnp.zeros((OWNERS, *own.shape[1:]), own.dtype)
    held = lax.dynamic_update_slice_in_dim(held, own, 0, 0)
    for step in range(4):
        count = 1 << step
        arrived = exchange(held[:count], step)
        held = lax.dynamic_update_slice_in_dim(held, arrived, count, 0)
    return held


def reduce_halving(keep, away):
    held = keep.astype(F32) + swap_cores(away).astype(F32)
    for step in (3, 2, 1, 0):
        count = 1 << step
        held = held[:count] + exchange(held[count:].astype(BF), step).astype(F32)
    return held[0]


def reduce_general(send, weights, gathered, layer):
    total = jnp.stack([send[place_of(owner, layer)] for owner in range(OWNERS)]).astype(F32)

    def matrix(places):
        return jnp.concatenate([total[:, p : p + 8].reshape(D, 128) for p in places], axis=1)

    attn, up, proj = matrix((0, 8, 16)), matrix((32, 40, 48, 56)), matrix((24,))
    down = total[:, 64:96].reshape(FF, D)
    small, whole = total[:, 96:104].reshape(D, 128), total[0, 104:112]
    attn_w, up_w = gathered[0][layer].astype(F32), gathered[7][layer].astype(F32)
    again, ashift, fgain, fshift = (gathered[i][layer].astype(F32)[:, None] for i in (5, 6, 11, 12))
    attn_sum, up_sum = whole[0:3].reshape(1, 3 * D), whole[3:7].reshape(1, FF)
    up_bias = jnp.swapaxes(total[:, 96:104, 4:8], 1, 2).reshape(FF)
    local = (
        again * attn + ashift * attn_sum, small[:, 0], small[:, 1], proj, small[:, 2],
        jnp.sum(attn_w * attn, axis=1), jnp.sum(attn_w * attn_sum, axis=1),
        fgain * up + fshift * up_sum, up_bias, down, small[:, 3],
        jnp.sum(up_w * up, axis=1), jnp.sum(up_w * up_sum, axis=1),
    )
    return tuple(
        lax.psum_scatter(lax.psum(g, "dp"), "wide", scatter_dimension=0, tiled=True) for g in local
    )


def body(tokens, field_ids, seq_lengths, cotangent, *weights, owners):
    seqs = seq_lengths.shape[0]
    fields = field_ids.reshape(seqs, 1, -1)
    doubling = owners == OWNERS
    if doubling:
        shard, own = run_pack(weights)
        own = gather_doubling(own)
        other = swap_cores(own)
    else:
        gathered = [lax.all_gather(w, "wide", axis=1, tiled=True) for w in weights]
        packed = [pack_weights(gathered, layer, OWNERS) for layer in range(LAYERS)]
        places = [sorted(range(OWNERS), key=lambda owner: place_of(owner, core)) for core in range(2)]
        own, other = (jnp.stack([p[owner] for owner in order]) for p, order in zip(packed, places))
    output, token_grad, keep, away = run_layers(seq_lengths, tokens, fields, cotangent, own, other, doubling)
    if doubling:
        reduced = reduce_halving(keep, away)
        grads = run_finish(reduced, swap_cores(reduced), shard)
    else:
        by_layer = [reduce_general(send, weights, gathered, layer) for layer, send in enumerate((keep, away))]
        grads = [jnp.stack(pair) for pair in zip(*by_layer)]
    return (output, token_grad, *grads)


def solution(mesh):
    rows, vector = P(("dp", "wide"), None), P(("dp", "wide"))
    flat, square = P(None, "wide"), P(None, "wide", None)
    params = (square, flat, flat, square, flat, flat, flat, square, flat, square, flat, flat, flat)
    return jax.shard_map(
        functools.partial(body, owners=mesh.shape["wide"]),
        mesh=mesh,
        in_specs=(rows, vector, vector, rows, *params),
        out_specs=(rows, rows, *params),
        check_vma=False,
    )
```

```python
import functools
import math

import jax
import jax.numpy as jnp
from jax import lax
from jax.experimental import pallas as pl
from jax.experimental.pallas import tpu as pltpu
from jax.sharding import PartitionSpec as P

HEADS = 4
EPSILON = 1e-05
NEGATIVE = -1e30
BLOCK = 128
D = 128
FF = 512
OWNERS = 16
SHARD_ROWS = 104
GRAD_ROWS = 112
LAYERS = 2
GROUP = 2
SPAN = 256
CHUNK = 256
VMEM_BYTES = 50 * 2**20

BF = jnp.bfloat16
F32 = jnp.float32
NN = (((1,), (0,)), ((), ()))


def dot(a, b):
    return lax.dot_general(a, b, NN, preferred_element_type=F32)


def flip(x):
    return jnp.transpose(x)


def col(vec_ref, index):
    return vec_ref[:, index : index + 1]


STEP_BITS = ((8, 4, 2, 1), (4, 8, 1, 2))


def place_of(relative, core):
    first = ((relative & 1) << 3) | ((relative & 2) << 1) | ((relative & 4) >> 1) | ((relative & 8) >> 3)
    return first if core == 0 else ((first & 5) << 1) | ((first & 10) >> 1)


def place_by(relative, core):
    return jnp.where(core == 0, place_of(relative, 0), place_of(relative, 1))


def position(known):
    return (lax.axis_index("wide"), lax.axis_index("dp")) if known else (jnp.int32(0), jnp.int32(0))


def unpack(me, core, packed_ref, stage):
    for owner in range(OWNERS):
        stage[owner] = packed_ref[place_by(jnp.bitwise_xor(me, owner), core)].astype(F32)


def stage_rows(stage, start, count):
    return stage[:, start : start + count, :].reshape(OWNERS * count, 128)


def unpack_forward(stage, qkv_t, proj_t, up_t, down_t):
    for part in range(3):
        qkv_t[part * D : (part + 1) * D, :] = flip(stage_rows(stage, 8 * part, 8)).astype(BF)
    proj_t[...] = flip(stage_rows(stage, 24, 8)).astype(BF)
    for part in range(4):
        up_t[part * D : (part + 1) * D, :] = flip(stage_rows(stage, 32 + 8 * part, 8)).astype(BF)
    down_t[...] = flip(stage_rows(stage, 64, 32)).astype(BF)


def unpack_backward(stage, qkv, proj, up, down):
    for part in range(3):
        qkv[:, part * D : (part + 1) * D] = stage_rows(stage, 8 * part, 8).astype(BF)
    proj[...] = stage_rows(stage, 24, 8).astype(BF)
    for part in range(4):
        up[:, part * D : (part + 1) * D] = stage_rows(stage, 32 + 8 * part, 8).astype(BF)
    down[...] = stage_rows(stage, 64, 32).astype(BF)


def unpack_vectors(stage, vec, up_bias):
    small = stage[:, 96:104, :]
    vec[...] = small.reshape(D, 128)
    for part in range(4):
        piece = small[:, :, 8 + part : 9 + part]
        up_bias[:, part, :, :] = jnp.broadcast_to(piece, (OWNERS, 8, 128))


QUERY_BIAS, VALUE_BIAS, PROJ_BIAS, ATTN_GAIN, ATTN_SHIFT, DOWN_BIAS, FFN_GAIN, FFN_SHIFT = range(8)


def norm_stats(x):
    mean = jnp.mean(x, axis=0, keepdims=True)
    centred = x - mean
    spread = jnp.mean(centred * centred, axis=0, keepdims=True)
    rstd = lax.rsqrt(spread + EPSILON)
    return centred * rstd, rstd


def norm_backward(grad_out, gain, unit, rstd):
    weighted = grad_out * gain
    first = jnp.mean(weighted, axis=0, keepdims=True)
    second = jnp.mean(weighted * unit, axis=0, keepdims=True)
    return rstd * (weighted - first - unit * second)


def head_columns(x, block, heads):
    size = D // HEADS
    piece = x[:, block * BLOCK : (block + 1) * BLOCK]
    columns = []
    for head in heads:
        rows = [
            piece[head * size : (head + 1) * size] if other == head else jnp.zeros((size, BLOCK), piece.dtype)
            for other in range(HEADS)
        ]
        columns.append(jnp.concatenate(rows, axis=0))
    return jnp.concatenate(columns, axis=1)


def head_rows(x, block, heads):
    size = D // HEADS
    piece = x[block * BLOCK : (block + 1) * BLOCK, :]
    lane = lax.broadcasted_iota(jnp.int32, (BLOCK, D), 1) // size
    return jnp.concatenate([jnp.where(lane == head, piece, jnp.zeros_like(piece)) for head in heads], axis=0)


def own_columns(x, heads):
    size = D // HEADS
    return jnp.concatenate(
        [x[head * size : (head + 1) * size, at * BLOCK : (at + 1) * BLOCK] for at, head in enumerate(heads)], axis=0
    )


def head_spread(rows):
    size = D // HEADS
    return jnp.concatenate(
        [jnp.broadcast_to(rows[head : head + 1], (size, rows.shape[1])) for head in range(HEADS)], axis=0
    )


def extra_rows(rows, total=D):
    width = rows[0].shape[1]
    filled = jnp.zeros((16, width), F32)
    place = lax.broadcasted_iota(jnp.int32, (16, width), 0)
    for index, row in enumerate(rows):
        filled = jnp.where(place == index, jnp.broadcast_to(row, (16, width)), filled)
    return jnp.concatenate([filled.astype(BF), jnp.zeros((total - 16, width), BF)], axis=0)


PAIRS = ((0, 1, 2, 3),)


def attend_forward(x, key_bias, own_bias, w, save):
    qkv_t, _, _, _, vec, _ = w
    tokens = x.shape[1]
    blocks = tokens // BLOCK
    size = D // HEADS
    unit, rstd = norm_stats(x)
    normed = (unit * col(vec, ATTN_GAIN) + col(vec, ATTN_SHIFT)).astype(BF)
    save["unit"][...] = unit.astype(BF)
    save["rows"][0:1] = rstd
    yield
    factor = size ** (-0.5) / math.log(2.0)
    query = ((dot(qkv_t[:D], normed) + col(vec, QUERY_BIAS)) * factor).astype(BF)
    save["query"][...] = query
    yield
    key = dot(qkv_t[D : 2 * D], normed).astype(BF)
    save["key"][...] = key
    key_plain = flip(key)
    key_rows = jnp.concatenate([key_plain, key_bias], axis=1)
    yield
    value = (dot(qkv_t[2 * D :], normed) + col(vec, VALUE_BIAS)).astype(BF)
    save["value"][...] = value
    value_ones = jnp.concatenate([value, jnp.ones((16, tokens), BF)], axis=0)
    ones = extra_rows([jnp.ones((1, len(PAIRS[0]) * BLOCK), F32)])
    for block in range(blocks):
        seen = (block + 1) * BLOCK
        at = slice(block * BLOCK, seen)
        for pair, heads in enumerate(PAIRS):
            yield
            columns = head_columns(query, block, heads)
            scores = dot(key_plain[seen - BLOCK : seen], columns) + jnp.concatenate([own_bias[block]] * len(heads), axis=1)
            if block:
                right = jnp.concatenate([columns, ones], axis=0)
                scores = jnp.concatenate([dot(key_rows[: seen - BLOCK], right), scores], axis=0)
            raised = jnp.exp2(scores - jnp.max(scores, axis=0, keepdims=True)).astype(BF)
            save["probs"][block][:, pair * len(heads) * BLOCK : (pair + 1) * len(heads) * BLOCK] = raised
            yield
            summed = dot(value_ones[:, :seen], raised)
            total = summed[D : D + 1]
            inv = 1.0 / total
            for place, head in enumerate(heads):
                save["rows"][2 + head : 3 + head, at] = inv[:, place * BLOCK : (place + 1) * BLOCK]
            save["attended"][heads[0] * size : (heads[-1] + 1) * size, at] = own_columns(summed[:D] * inv, heads)


def feed_forward(x, w, save):
    _, proj_t, up_t, down_t, vec, up_bias = w
    tokens = x.shape[1]
    middle = x + (dot(proj_t[...], save["attended"][...].astype(BF)) + col(vec, PROJ_BIAS))
    yield
    unit_two, rstd_two = norm_stats(middle)
    save["unit_two"][...] = unit_two.astype(BF)
    save["rows"][1:2] = rstd_two
    normed_two = (unit_two * col(vec, FFN_GAIN) + col(vec, FFN_SHIFT)).astype(BF)
    root = math.sqrt(2.0 / math.pi)
    result = []
    for start in range(0, tokens, SPAN):
        at = slice(start, start + SPAN)
        for row in range(0, FF, CHUNK):
            yield
            rows = slice(row, row + CHUNK)
            bias = jnp.concatenate([up_bias[rows]] * (SPAN // 128), axis=1)
            expanded = dot(up_t[rows], normed_two[:, at]) + bias
            square = expanded * expanded
            bent = jnp.tanh(expanded * (root + (root * 0.044715) * square))
            half = 0.5 + 0.5 * bent
            active = expanded * half
            save["active"][rows, at] = active.astype(BF)
            slope = half + active * ((1.0 - bent) * (root + (3.0 * root * 0.044715) * square))
            save["slope"][rows, at] = slope.astype(BF)
        yield
        result.append(middle[:, at] + col(vec, DOWN_BIAS) + dot(down_t[...], save["active"][:, at]))
    return jnp.concatenate(result, axis=1)


def feed_backward(grad, grad_rows, w, kept, total):
    _, _, up, down, vec = w
    tokens = grad.shape[1]
    grad_low = grad.astype(BF)
    for start in range(0, tokens, SPAN):
        at = slice(start, start + SPAN)
        for row in range(0, FF, CHUNK):
            rows = slice(row, row + CHUNK)
            grad_active = dot(down[rows], grad_low[:, at])
            kept["slope"][rows, at] = (grad_active * kept["slope"][rows, at].astype(F32)).astype(BF)
            yield
    unit_two = kept["unit_two"][...]
    normed = dot(up[...], kept["slope"][...])
    yield
    lane = lax.broadcasted_iota(jnp.int32, (tokens, D), 1)
    ones_lane = jnp.where(lane == 0, 1.0, 0.0).astype(BF)
    unit_two_rows = jnp.concatenate([flip(unit_two), ones_lane], axis=1)
    for row in range(0, FF, CHUNK):
        rows = slice(row, row + CHUNK)
        total["down"][rows] += dot(kept["active"][rows], grad_rows)
        yield
        total["up"][rows] += dot(kept["slope"][rows], unit_two_rows)
        yield
    total["down_bias"][...] += dot(jnp.ones((16, tokens), BF), grad_rows)[:8]
    return grad + norm_backward(normed, col(vec, FFN_GAIN), unit_two.astype(F32), kept["rows"][1:2])


def attend_backward(grad_middle, w, kept, total):
    qkv, proj, _, _, vec = w
    tokens = grad_middle.shape[1]
    blocks = tokens // BLOCK
    size = D // HEADS
    ones_row = jnp.ones((16, tokens), BF)
    lane = lax.broadcasted_iota(jnp.int32, (tokens, D), 1)
    grad_proj = grad_middle.astype(BF)
    attended = kept["attended"][...]
    total["proj"][...] += dot(jnp.concatenate([attended.astype(BF), ones_row], axis=0), flip(grad_proj))
    yield
    grad_attended = dot(proj[...], grad_proj).astype(BF).astype(F32)
    scaled = (grad_attended * head_spread(kept["rows"][2 : 2 + HEADS])).astype(BF)
    yield
    product = scaled.astype(F32) * attended
    centre = [jnp.sum(product[h * size : (h + 1) * size], axis=0, keepdims=True) for h in range(HEADS)]
    centre_high = [c.astype(BF).astype(F32) for c in centre]
    centre_low = [c - high for c, high in zip(centre, centre_high)]
    minus = jnp.where(lane < 2, -1.0, 0.0).astype(BF)
    value_rows = jnp.concatenate([flip(kept["value"][...]), minus], axis=1)
    key = kept["key"][...]
    query_rows = flip(kept["query"][...])
    scaled_rows = flip(scaled)
    grad_query = []
    grad_value = [None] * blocks
    grad_key = [None] * blocks

    def gather_row(parts, block, heads):
        return jnp.concatenate([parts[h][:, block * BLOCK : (block + 1) * BLOCK] for h in heads], axis=1)

    for block in range(blocks):
        seen = (block + 1) * BLOCK
        for pair, heads in enumerate(PAIRS):
            yield
            right = jnp.concatenate(
                [
                    head_columns(scaled, block, heads),
                    extra_rows([gather_row(centre_high, block, heads), gather_row(centre_low, block, heads)]),
                ],
                axis=0,
            )
            grad_probs = dot(value_rows[:seen], right)
            raised = kept["probs"][block][:, pair * len(heads) * BLOCK : (pair + 1) * len(heads) * BLOCK]
            grad_scores = raised * grad_probs.astype(BF)
            yield
            grad_query.append(own_columns(dot(key[:, :seen], grad_scores), heads))
            yield
            value_part = dot(raised, head_rows(scaled_rows, block, heads))
            for j in range(block + 1):
                v = value_part[j * BLOCK : (j + 1) * BLOCK]
                grad_value[j] = v if grad_value[j] is None else grad_value[j] + v
            yield
            key_part = dot(grad_scores, head_rows(query_rows, block, heads))
            for j in range(block + 1):
                k = key_part[j * BLOCK : (j + 1) * BLOCK]
                grad_key[j] = k if grad_key[j] is None else grad_key[j] + k
    yield
    grad_query = [jnp.concatenate(grad_query[len(PAIRS) * block : len(PAIRS) * (block + 1)], axis=0) for block in range(blocks)]
    grad_query = (jnp.concatenate(grad_query, axis=1) * size ** (-0.5)).astype(BF)
    grad_key = (jnp.concatenate(grad_key, axis=0) * math.log(2.0)).astype(BF)
    grad_value = jnp.concatenate(grad_value, axis=0).astype(BF)
    packed_rows = jnp.concatenate([flip(grad_query), grad_key, grad_value], axis=1)
    packed = jnp.concatenate([grad_query, flip(grad_key), flip(grad_value)], axis=0)
    yield
    unit = kept["unit"][...]
    total["qkv"][...] += dot(jnp.concatenate([unit, ones_row], axis=0), packed_rows)
    yield
    grad_normed = dot(qkv[...], packed)
    return grad_middle + norm_backward(grad_normed, col(vec, ATTN_GAIN), unit.astype(F32), kept["rows"][0:1])


def pack_grads(me, core, total, send):
    qkv, proj, up, down, down_bias = (total[n] for n in ("qkv", "proj", "up", "down", "down_bias"))
    up_t = [flip(up[D * part : D * (part + 1), :D]) for part in range(4)]
    up_sum = up[:, D:]
    up_sum_rows = [flip(up_sum[D * part : D * (part + 1)])[0:1] for part in range(4)]
    sums = jnp.concatenate(
        [
            qkv[D : D + 1, :D],
            qkv[D : D + 1, 2 * D : 3 * D],
            proj[D : D + 1],
            down_bias[0:1],
            jnp.zeros((D - 4, D), F32),
        ],
        axis=0,
    )
    columns = flip(sums)
    lane = lax.broadcasted_iota(jnp.int32, (8, 128), 1)
    whole = jnp.concatenate(
        [qkv[D : D + 1, D * part : D * (part + 1)] for part in range(3)]
        + up_sum_rows
        + [jnp.zeros((1, D), F32)],
        axis=0,
    )
    for owner in range(OWNERS):
        own = slice(8 * owner, 8 * owner + 8)
        small = jnp.where(lane < 4, columns[own], 0.0)
        for part in range(4):
            at = 32 * owner + 8 * part
            small = jnp.where(lane == 4 + part, jnp.broadcast_to(up_sum[at : at + 8, 0:1], (8, 128)), small)
        pieces = (
            [qkv[own, D * part : D * (part + 1)] for part in range(3)]
            + [proj[own]]
            + [u[own] for u in up_t]
            + [down[32 * owner : 32 * owner + 32], small, whole]
        )
        send[place_by(jnp.bitwise_xor(me, owner), core)] = jnp.concatenate(pieces, axis=0).astype(BF)


KEPT = ("unit", "query", "key", "value", "attended", "unit_two", "rows", "active", "slope")


def kept_shapes(tokens):
    shapes = {name: ((D, tokens), BF) for name in KEPT}
    shapes["rows"] = ((8, tokens), F32)
    shapes["attended"] = ((D, tokens), F32)
    shapes["active"] = ((FF, tokens), BF)
    shapes["slope"] = ((FF, tokens), BF)
    for block in range(tokens // BLOCK):
        shapes[f"probs{block}"] = (((block + 1) * BLOCK, HEADS * BLOCK), BF)
    return shapes


def as_kept(names, refs):
    kept = dict(zip(names, refs))
    probs = [kept.pop(n) for n in names if n.startswith("probs")]
    kept["probs"] = probs
    return kept


FORWARD_SCRATCH = [
    pltpu.VMEM((LAYERS, 3 * D, D), BF),
    pltpu.VMEM((LAYERS, D, D), BF),
    pltpu.VMEM((LAYERS, FF, D), BF),
    pltpu.VMEM((LAYERS, D, FF), BF),
]
BACKWARD_SCRATCH = [
    pltpu.VMEM((LAYERS, D, 3 * D), BF),
    pltpu.VMEM((LAYERS, D, D), BF),
    pltpu.VMEM((LAYERS, D, FF), BF),
    pltpu.VMEM((LAYERS, FF, D), BF),
]
VECTOR_SCRATCH = [
    pltpu.VMEM((LAYERS, OWNERS, SHARD_ROWS, 128), F32),
    pltpu.VMEM((LAYERS, D, 128), F32),
    pltpu.VMEM((LAYERS, OWNERS, 4, 8, 128), F32),
]
TOTALS = ("qkv", "proj", "up", "down", "down_bias")
TOTAL_SCRATCH = [
    pltpu.VMEM((LAYERS, D + 16, 3 * D), F32),
    pltpu.VMEM((LAYERS, D + 16, D), F32),
    pltpu.VMEM((LAYERS, FF, 2 * D), F32),
    pltpu.VMEM((LAYERS, FF, D), F32),
    pltpu.VMEM((LAYERS, 8, D), F32),
]


def key_bias_rows(field_row, length):
    tokens = field_row.shape[1]
    at = lax.broadcasted_iota(jnp.int32, (1, tokens), 1)
    shut = jnp.where(field_row == 0, NEGATIVE, jnp.where(at >= length, NEGATIVE, 0.0))
    place = lax.broadcasted_iota(jnp.int32, (16, tokens), 0)
    rows = jnp.where(place == 0, jnp.broadcast_to(shut, (16, tokens)), 0.0)
    columns = flip(rows)
    low = jnp.concatenate([columns, jnp.zeros((tokens, D - 16), F32)], axis=1).astype(BF)
    key_at = lax.broadcasted_iota(jnp.int32, (BLOCK, BLOCK), 0)
    query_at = lax.broadcasted_iota(jnp.int32, (BLOCK, BLOCK), 1)
    own = []
    for block in range(tokens // BLOCK):
        column = jnp.broadcast_to(columns[block * BLOCK : (block + 1) * BLOCK, 0:1], (BLOCK, BLOCK))
        own.append(jnp.where(key_at < query_at, column, jnp.where(key_at == query_at, 0.0, NEGATIVE)))
    return low, own


FORWARD_STEPS = (12, 8)
BACKWARD_STEPS = (10, 21)


def groups_of(seqs):
    sizes = [GROUP] * (seqs // GROUP)
    if seqs % GROUP:
        sizes.insert(max(len(sizes) - 1, 0), seqs % GROUP)
    ends = [sum(sizes[: g + 1]) for g in range(len(sizes))]
    return [list(range(end - size, end)) for end, size in zip(ends, sizes)]


def run_together(chains):
    results = [None] * len(chains)
    done = [0.0] * len(chains)
    rate = [[1.0 / steps for layer in range(LAYERS) for steps in phases for _ in range(steps)] for _, phases in chains]
    count = [0] * len(chains)
    live = list(range(len(chains)))
    while live:
        index = min(live, key=lambda i: done[i])
        try:
            next(chains[index][0])
            done[index] += rate[index][min(count[index], len(rate[index]) - 1)]
            count[index] += 1
        except StopIteration as stop:
            results[index] = stop.value
            live.remove(index)
    return results


def layers_kernel(
    names, known, length_ref, tokens_ref, field_ref, cot_ref, own_ref, other_ref, output_ref, grad_ref, keep_ref, away_ref, *scratch
):
    forward, backward, (stage, vec, up_bias) = scratch[:4], scratch[4:8], scratch[8:11]
    totals, kept = scratch[11:16], scratch[16:]
    seqs, tokens = field_ref.shape[0], field_ref.shape[2]
    me, core = position(known)
    unpack(me, core, own_ref, stage.at[core])
    unpack(me, 1 - core, other_ref, stage.at[1 - core])

    def total_of(layer):
        return dict(zip(TOTALS, [ref.at[layer] for ref in totals]))

    total = [total_of(layer) for layer in range(LAYERS)]
    for layer in range(LAYERS):
        unpack_forward(stage.at[layer], *[ref.at[layer] for ref in forward])
        unpack_backward(stage.at[layer], *[ref.at[layer] for ref in backward])
        unpack_vectors(stage.at[layer], vec.at[layer], up_bias.at[layer])

    def clear():
        for ref in totals:
            ref[...] = jnp.zeros_like(ref)

    def saved(slot, layer):
        n=len(names)
        return as_kept(names, [ref.at[layer] for ref in kept[slot*n:(slot+1)*n]])

    def rows_of(seq):
        return pl.ds(pl.multiple_of(seq * tokens, tokens), tokens)

    def forward_chain(seq, slot):
        bias, own_bias = key_bias_rows(field_ref[seq], length_ref[seq])
        state = flip(tokens_ref[rows_of(seq), :]).astype(F32)
        for layer in range(LAYERS):
            w = (*[ref.at[layer] for ref in forward], vec.at[layer], up_bias[layer].reshape(FF, 128))
            save = saved(slot, layer)
            yield from attend_forward(state, bias, own_bias, w, save)
            yield
            state = yield from feed_forward(state, w, save)
            yield
        output_ref[rows_of(seq), :] = flip(state.astype(BF))

    def backward_chain(seq, slot):
        grad_rows = cot_ref[rows_of(seq), :]
        grad = flip(grad_rows).astype(F32)
        for layer in reversed(range(LAYERS)):
            w = (*[ref.at[layer] for ref in backward], vec.at[layer])
            save = saved(slot, layer)
            if layer < LAYERS - 1:
                grad_rows = flip(grad.astype(BF))
            grad = yield from feed_backward(grad, grad_rows, w, save, total[layer])
            yield
            grad = yield from attend_backward(grad, w, save, total[layer])
            yield
        grad_ref[rows_of(seq), :] = flip(grad)

    clear()
    before = []
    for group in groups_of(seqs) + [[]]:
        used = [slot for _, slot in before]
        free = [slot for slot in range(2 * seqs) if slot not in used]
        now = list(zip(group, free))
        run_together(
            [(backward_chain(jnp.int32(seq), slot), BACKWARD_STEPS) for seq, slot in before]
            + [(forward_chain(jnp.int32(seq), slot), FORWARD_STEPS) for seq, slot in now]
        )
        before = now

    pack_grads(me, core, total_of(core), keep_ref)
    pack_grads(me, 1 - core, total_of(1 - core), away_ref)


def near(x):
    return pltpu.with_memory_space_constraint(x, pltpu.VMEM)


def run_layers(lengths, tokens, fields, cotangent, own, other, known):
    seqs, _, length = fields.shape
    shapes = kept_shapes(length)
    sizes = [len(group) for group in groups_of(seqs)]
    slots = max(a + b for a, b in zip(sizes, sizes[1:] + [0]))
    smem, vmem = pl.BlockSpec(memory_space=pltpu.SMEM), pl.BlockSpec(memory_space=pltpu.VMEM)
    send = pltpu.VMEM((OWNERS, GRAD_ROWS, 128), BF)
    own, other, tokens, cotangent = near(own), near(other), near(tokens), near(cotangent)
    return pl.pallas_call(
        functools.partial(layers_kernel, tuple(shapes), known),
        in_specs=[smem] + [vmem] * 5,
        out_specs=[vmem] * 4,
        out_shape=[
            pltpu.VMEM(tokens.shape, BF),
            pltpu.VMEM(tokens.shape, F32),
            send,
            send,
        ],
        scratch_shapes=FORWARD_SCRATCH
        + BACKWARD_SCRATCH
        + VECTOR_SCRATCH
        + TOTAL_SCRATCH
        + [pltpu.VMEM((LAYERS, *shape), dtype) for _ in range(slots) for shape, dtype in shapes.values()],
        compiler_params=pltpu.CompilerParams(vmem_limit_bytes=VMEM_BYTES),
        name="layers",
    )(lengths, tokens, fields, cotangent, own, other)


def pack_kernel(attn, qb, vb, proj, pb, ag, ash, up, ub, down, db, fg, fsh, shard_ref, own_ref):
    for layer in range(LAYERS):
        one = slice(layer, layer + 1)
        rows = [ref[one].astype(F32) for ref in (qb, vb, pb, ag, ash, db, fg, fsh)]
        bias = ub[one].astype(F32)
        rows += [bias[:, 8 * part : 8 * part + 8] for part in range(4)] + [jnp.zeros((4, 8), F32)]
        rows = jnp.concatenate(rows, axis=0)
        rows = jnp.concatenate([rows, jnp.zeros((16, 120), F32)], axis=1)
        small = flip(jnp.concatenate([rows, jnp.zeros((112, 128), F32)], axis=0))[:8]
        pieces = []
        for ref in (attn, proj, up):
            matrix = ref[layer].astype(F32)
            pieces += [matrix[:, 128 * part : 128 * (part + 1)] for part in range(matrix.shape[1] // 128)]
        shard_ref[layer] = jnp.concatenate(pieces + [down[layer].astype(F32), small], axis=0).astype(BF)
    own_ref[0] = shard_ref[lax.axis_index("dp")]


def run_pack(weights):
    vmem = pl.BlockSpec(memory_space=pltpu.VMEM)
    return pl.pallas_call(
        pack_kernel,
        in_specs=[vmem] * 13,
        out_specs=[vmem] * 2,
        out_shape=[
            jax.ShapeDtypeStruct((LAYERS, SHARD_ROWS, 128), BF),
            pltpu.VMEM((1, SHARD_ROWS, 128), BF),
        ],
        name="pack",
    )(*weights)


def finish_kernel(own_ref, other_ref, shard_ref, *outs):
    (attn, query_bias, value_bias, proj, proj_bias, attn_gain, attn_shift, up, up_bias, down, down_bias, ffn_gain, ffn_shift) = outs
    lane = lax.broadcasted_iota(jnp.int32, (8, 128), 1)
    for layer in range(LAYERS):
        red = jnp.where(lax.axis_index("dp") == layer, own_ref[...], other_ref[...])
        own = shard_ref[layer].astype(F32)
        small_in = own[96:104]
        small, whole = red[96:104], red[104:112]
        gains = [None, None]
        shifts = [None, None]
        for index, (places, gain_at, shift_at, target) in enumerate(
            (((0, 8, 16), ATTN_GAIN, ATTN_SHIFT, attn), ((32, 40, 48, 56), FFN_GAIN, FFN_SHIFT, up))
        ):
            gain, shift = small_in[:, gain_at : gain_at + 1], small_in[:, shift_at : shift_at + 1]
            first = 0 if index == 0 else 3
            gain_sum = jnp.zeros((8, 128), F32)
            shift_sum = jnp.zeros((8, 128), F32)
            for part, place in enumerate(places):
                grad, weight = red[place : place + 8], own[place : place + 8]
                column_sum = whole[first + part : first + part + 1]
                target[layer, :, 128 * part : 128 * (part + 1)] = gain * grad + shift * column_sum
                gain_sum += weight * grad
                shift_sum += weight * column_sum
            gains[index] = jnp.sum(gain_sum, axis=1, keepdims=True)
            shifts[index] = jnp.sum(shift_sum, axis=1, keepdims=True)
        proj[layer] = red[24:32]
        down[layer] = red[64:96]
        for at, column in ((8, gains[0]), (9, shifts[0]), (10, gains[1]), (11, shifts[1])):
            small = jnp.where(lane == at, jnp.broadcast_to(column, (8, 128)), small)
        rows = flip(small)
        query_bias[layer : layer + 1] = rows[0:1]
        value_bias[layer : layer + 1] = rows[1:2]
        proj_bias[layer : layer + 1] = rows[2:3]
        down_bias[layer : layer + 1] = rows[3:4]
        up_bias[layer : layer + 1] = jnp.concatenate([rows[4 + part : 5 + part] for part in range(4)], axis=1)
        attn_gain[layer : layer + 1] = rows[8:9]
        attn_shift[layer : layer + 1] = rows[9:10]
        ffn_gain[layer : layer + 1] = rows[10:11]
        ffn_shift[layer : layer + 1] = rows[11:12]


def run_finish(own, other, shard):
    layers = LAYERS
    vector = jax.ShapeDtypeStruct((layers, 8), F32)

    def matrix(rows, columns):
        return jax.ShapeDtypeStruct((layers, rows, columns), F32)

    shapes = [
        matrix(8, 3 * D), vector, vector, matrix(8, D), vector, vector, vector, matrix(8, FF),
        jax.ShapeDtypeStruct((layers, 32), F32), matrix(32, D), vector, vector, vector,
    ]
    return pl.pallas_call(
        finish_kernel,
        in_specs=[pl.BlockSpec(memory_space=pltpu.VMEM)] * 3,
        out_specs=[pl.BlockSpec(memory_space=pltpu.VMEM)] * len(shapes),
        out_shape=shapes,
        name="finish",
    )(near(own), near(other), shard)


def pack_weights(weights, layer, owners):
    attn, qb, vb, proj, pb, ag, ash, up, ub, down, db, fg, fsh = (w[layer] for w in weights)

    def blocks(matrix, count):
        return [matrix[:, 128 * part : 128 * (part + 1)].reshape(owners, 8, 128) for part in range(count)]

    vectors = [v.reshape(owners, 8, 1) for v in (qb, vb, pb, ag, ash, db, fg, fsh)]
    bias = jnp.swapaxes(ub.reshape(owners, 4, 8), 1, 2)
    small = jnp.concatenate(vectors + [bias], axis=2)
    small = jnp.pad(small, ((0, 0), (0, 0), (0, 128 - small.shape[2])))
    return jnp.concatenate(
        blocks(attn, 3) + blocks(proj, 1) + blocks(up, 4) + [down.reshape(owners, 32, 128), small], axis=1
    )


def exchange(x, step):
    pairs = [
        (core * OWNERS + i, core * OWNERS + (i ^ bits[step])) for core, bits in enumerate(STEP_BITS) for i in range(OWNERS)
    ]
    return lax.ppermute(x, ("dp", "wide"), pairs)


def swap_cores(x):
    return lax.ppermute(x, "dp", [(0, 1), (1, 0)])


def gather_doubling(own):
    held = jnp.zeros((OWNERS, *own.shape[1:]), own.dtype)
    held = lax.dynamic_update_slice_in_dim(held, own, 0, 0)
    for step in range(4):
        count = 1 << step
        arrived = exchange(held[:count], step)
        held = lax.dynamic_update_slice_in_dim(held, arrived, count, 0)
    return held


def reduce_halving(keep, away):
    held = keep.astype(F32) + swap_cores(away).astype(F32)
    for step in (3, 2, 1, 0):
        count = 1 << step
        held = held[:count] + exchange(held[count:].astype(BF), step).astype(F32)
    return held[0]


def reduce_general(send, weights, gathered, layer):
    total = jnp.stack([send[place_of(owner, layer)] for owner in range(OWNERS)]).astype(F32)

    def matrix(places):
        return jnp.concatenate([total[:, p : p + 8].reshape(D, 128) for p in places], axis=1)

    attn, up, proj = matrix((0, 8, 16)), matrix((32, 40, 48, 56)), matrix((24,))
    down = total[:, 64:96].reshape(FF, D)
    small, whole = total[:, 96:104].reshape(D, 128), total[0, 104:112]
    attn_w, up_w = gathered[0][layer].astype(F32), gathered[7][layer].astype(F32)
    again, ashift, fgain, fshift = (gathered[i][layer].astype(F32)[:, None] for i in (5, 6, 11, 12))
    attn_sum, up_sum = whole[0:3].reshape(1, 3 * D), whole[3:7].reshape(1, FF)
    up_bias = jnp.swapaxes(total[:, 96:104, 4:8], 1, 2).reshape(FF)
    local = (
        again * attn + ashift * attn_sum, small[:, 0], small[:, 1], proj, small[:, 2],
        jnp.sum(attn_w * attn, axis=1), jnp.sum(attn_w * attn_sum, axis=1),
        fgain * up + fshift * up_sum, up_bias, down, small[:, 3],
        jnp.sum(up_w * up, axis=1), jnp.sum(up_w * up_sum, axis=1),
    )
    return tuple(
        lax.psum_scatter(lax.psum(g, "dp"), "wide", scatter_dimension=0, tiled=True) for g in local
    )


def body(tokens, field_ids, seq_lengths, cotangent, *weights, owners):
    seqs = seq_lengths.shape[0]
    fields = field_ids.reshape(seqs, 1, -1)
    doubling = owners == OWNERS
    if doubling:
        shard, own = run_pack(weights)
        own = gather_doubling(own)
        other = swap_cores(own)
    else:
        gathered = [lax.all_gather(w, "wide", axis=1, tiled=True) for w in weights]
        packed = [pack_weights(gathered, layer, OWNERS) for layer in range(LAYERS)]
        places = [sorted(range(OWNERS), key=lambda owner: place_of(owner, core)) for core in range(2)]
        own, other = (jnp.stack([p[owner] for owner in order]) for p, order in zip(packed, places))
    output, token_grad, keep, away = run_layers(seq_lengths, tokens, fields, cotangent, own, other, doubling)
    if doubling:
        reduced = reduce_halving(keep, away)
        grads = run_finish(reduced, swap_cores(reduced), shard)
    else:
        by_layer = [reduce_general(send, weights, gathered, layer) for layer, send in enumerate((keep, away))]
        grads = [jnp.stack(pair) for pair in zip(*by_layer)]
    return (output, token_grad, *grads)


def solution(mesh):
    rows, vector = P(("dp", "wide"), None), P(("dp", "wide"))
    flat, square = P(None, "wide"), P(None, "wide", None)
    params = (square, flat, flat, square, flat, flat, flat, square, flat, square, flat, flat, flat)
    return jax.shard_map(
        functools.partial(body, owners=mesh.shape["wide"]),
        mesh=mesh,
        in_specs=(rows, vector, vector, rows, *params),
        out_specs=(rows, rows, *params),
        check_vma=False,
    )
```

```python
import functools
import math

import jax
import jax.numpy as jnp
from jax import lax
from jax.experimental import pallas as pl
from jax.experimental.pallas import tpu as pltpu
from jax.sharding import PartitionSpec as P

HEADS = 4
EPSILON = 1e-05
NEGATIVE = -1e30
BLOCK = 128
D = 128
FF = 512
OWNERS = 16
SHARD_ROWS = 104
GRAD_ROWS = 112
LAYERS = 2
GROUP = 2
SPAN = 256
CHUNK = 256
VMEM_BYTES = 50 * 2**20
AGAIN_VMEM_BYTES = 36 * 2**20

BF = jnp.bfloat16
F32 = jnp.float32
NN = (((1,), (0,)), ((), ()))


def dot(a, b):
    return lax.dot_general(a, b, NN, preferred_element_type=F32)


def flip(x):
    return jnp.transpose(x)


def col(vec_ref, index):
    return vec_ref[:, index : index + 1]


STEP_BITS = ((8, 4, 2, 1), (4, 8, 1, 2))


def place_of(relative, core):
    first = ((relative & 1) << 3) | ((relative & 2) << 1) | ((relative & 4) >> 1) | ((relative & 8) >> 3)
    return first if core == 0 else ((first & 5) << 1) | ((first & 10) >> 1)


def place_by(relative, core):
    return jnp.where(core == 0, place_of(relative, 0), place_of(relative, 1))


def position(known):
    return (lax.axis_index("wide"), lax.axis_index("dp")) if known else (jnp.int32(0), jnp.int32(0))


def unpack(me, core, packed_ref, stage):
    for owner in range(OWNERS):
        stage[owner] = packed_ref[place_by(jnp.bitwise_xor(me, owner), core)].astype(F32)


def stage_rows(stage, start, count):
    return stage[:, start : start + count, :].reshape(OWNERS * count, 128)


def unpack_forward(stage, qkv_t, proj_t, up_t, down_t):
    for part in range(3):
        qkv_t[part * D : (part + 1) * D, :] = flip(stage_rows(stage, 8 * part, 8)).astype(BF)
    proj_t[...] = flip(stage_rows(stage, 24, 8)).astype(BF)
    for part in range(4):
        up_t[part * D : (part + 1) * D, :] = flip(stage_rows(stage, 32 + 8 * part, 8)).astype(BF)
    down_t[...] = flip(stage_rows(stage, 64, 32)).astype(BF)


def unpack_backward(stage, qkv, proj, up, down):
    for part in range(3):
        qkv[:, part * D : (part + 1) * D] = stage_rows(stage, 8 * part, 8).astype(BF)
    proj[...] = stage_rows(stage, 24, 8).astype(BF)
    for part in range(4):
        up[:, part * D : (part + 1) * D] = stage_rows(stage, 32 + 8 * part, 8).astype(BF)
    down[...] = stage_rows(stage, 64, 32).astype(BF)


def unpack_vectors(stage, vec, up_bias):
    small = stage[:, 96:104, :]
    vec[...] = small.reshape(D, 128)
    for part in range(4):
        piece = small[:, :, 8 + part : 9 + part]
        up_bias[:, part, :, :] = jnp.broadcast_to(piece, (OWNERS, 8, 128))


QUERY_BIAS, VALUE_BIAS, PROJ_BIAS, ATTN_GAIN, ATTN_SHIFT, DOWN_BIAS, FFN_GAIN, FFN_SHIFT = range(8)


def norm_stats(x):
    mean = jnp.mean(x, axis=0, keepdims=True)
    centred = x - mean
    spread = jnp.mean(centred * centred, axis=0, keepdims=True)
    rstd = lax.rsqrt(spread + EPSILON)
    return centred * rstd, rstd


def norm_backward(grad_out, gain, unit, rstd):
    weighted = grad_out * gain
    first = jnp.mean(weighted, axis=0, keepdims=True)
    second = jnp.mean(weighted * unit, axis=0, keepdims=True)
    return rstd * (weighted - first - unit * second)


def head_columns(x, block, heads):
    size = D // HEADS
    piece = x[:, block * BLOCK : (block + 1) * BLOCK]
    columns = []
    for head in heads:
        rows = [
            piece[head * size : (head + 1) * size] if other == head else jnp.zeros((size, BLOCK), piece.dtype)
            for other in range(HEADS)
        ]
        columns.append(jnp.concatenate(rows, axis=0))
    return jnp.concatenate(columns, axis=1)


def head_rows(x, block, heads):
    size = D // HEADS
    piece = x[block * BLOCK : (block + 1) * BLOCK, :]
    lane = lax.broadcasted_iota(jnp.int32, (BLOCK, D), 1) // size
    return jnp.concatenate([jnp.where(lane == head, piece, jnp.zeros_like(piece)) for head in heads], axis=0)


def own_columns(x, heads):
    size = D // HEADS
    return jnp.concatenate(
        [x[head * size : (head + 1) * size, at * BLOCK : (at + 1) * BLOCK] for at, head in enumerate(heads)], axis=0
    )


def head_spread(rows):
    size = D // HEADS
    return jnp.concatenate(
        [jnp.broadcast_to(rows[head : head + 1], (size, rows.shape[1])) for head in range(HEADS)], axis=0
    )


def extra_rows(rows, total=D):
    width = rows[0].shape[1]
    filled = jnp.zeros((16, width), F32)
    place = lax.broadcasted_iota(jnp.int32, (16, width), 0)
    for index, row in enumerate(rows):
        filled = jnp.where(place == index, jnp.broadcast_to(row, (16, width)), filled)
    return jnp.concatenate([filled.astype(BF), jnp.zeros((total - 16, width), BF)], axis=0)


PAIRS = ((0, 1, 2, 3),)


def attend_forward(x, key_bias, own_bias, w, save, limits):
    qkv_t, _, _, _, vec, _ = w
    tokens = x.shape[1]
    blocks = tokens // BLOCK
    size = D // HEADS
    unit, rstd = norm_stats(x)
    normed = (unit * col(vec, ATTN_GAIN) + col(vec, ATTN_SHIFT)).astype(BF)
    save["unit"][...] = unit.astype(BF)
    save["rows"][0:1] = rstd
    yield
    factor = size ** (-0.5) / math.log(2.0)
    query = ((dot(qkv_t[:D], normed) + col(vec, QUERY_BIAS)) * factor).astype(BF)
    save["query"][...] = query
    yield
    key = dot(qkv_t[D : 2 * D], normed).astype(BF)
    save["key"][...] = key
    key_plain = flip(key)
    key_rows = jnp.concatenate([key_plain, key_bias], axis=1)
    yield
    value = (dot(qkv_t[2 * D :], normed) + col(vec, VALUE_BIAS)).astype(BF)
    save["value"][...] = value
    value_ones = jnp.concatenate([value, jnp.ones((16, tokens), BF)], axis=0)
    ones = extra_rows([jnp.ones((1, len(PAIRS[0]) * BLOCK), F32)])
    for block in range(blocks):
        seen = (block + 1) * BLOCK
        at = slice(block * BLOCK, seen)
        for pair, heads in enumerate(PAIRS):
            yield
            columns = head_columns(query, block, heads)
            scores = dot(key_plain[seen - BLOCK : seen], columns) + jnp.concatenate([own_bias[block]] * len(heads), axis=1)
            if block:
                right = jnp.concatenate([columns, ones], axis=0)
                scores = jnp.concatenate([dot(key_rows[: seen - BLOCK], right), scores], axis=0)
            if limits is None:
                scores = scores - jnp.max(scores, axis=0, keepdims=True)
            raised = jnp.exp2(scores).astype(BF)
            save["probs"][block][:, pair * len(heads) * BLOCK : (pair + 1) * len(heads) * BLOCK] = raised
            yield
            summed = dot(value_ones[:, :seen], raised)
            total = summed[D : D + 1]
            if limits is not None:
                limits[0:1] = jnp.minimum(limits[0:1], total)
                limits[1:2] = jnp.maximum(limits[1:2], total)
            inv = 1.0 / total
            for place, head in enumerate(heads):
                save["rows"][2 + head : 3 + head, at] = inv[:, place * BLOCK : (place + 1) * BLOCK]
            save["attended"][heads[0] * size : (heads[-1] + 1) * size, at] = own_columns(summed[:D] * inv, heads)


def feed_forward(x, w, save):
    _, proj_t, up_t, down_t, vec, up_bias = w
    tokens = x.shape[1]
    middle = x + (dot(proj_t[...], save["attended"][...].astype(BF)) + col(vec, PROJ_BIAS))
    yield
    unit_two, rstd_two = norm_stats(middle)
    save["unit_two"][...] = unit_two.astype(BF)
    save["rows"][1:2] = rstd_two
    normed_two = (unit_two * col(vec, FFN_GAIN) + col(vec, FFN_SHIFT)).astype(BF)
    root = math.sqrt(2.0 / math.pi)
    result = []
    for start in range(0, tokens, SPAN):
        at = slice(start, start + SPAN)
        for row in range(0, FF, CHUNK):
            yield
            rows = slice(row, row + CHUNK)
            bias = jnp.concatenate([up_bias[rows]] * (SPAN // 128), axis=1)
            expanded = dot(up_t[rows], normed_two[:, at]) + bias
            square = expanded * expanded
            bent = jnp.tanh(expanded * (root + (root * 0.044715) * square))
            half = 0.5 + 0.5 * bent
            active = expanded * half
            save["active"][rows, at] = active.astype(BF)
            slope = half + active * ((1.0 - bent) * (root + (3.0 * root * 0.044715) * square))
            save["slope"][rows, at] = slope.astype(BF)
        yield
        result.append(middle[:, at] + col(vec, DOWN_BIAS) + dot(down_t[...], save["active"][:, at]))
    return jnp.concatenate(result, axis=1)


def feed_backward(grad, grad_rows, w, kept, total):
    _, _, up, down, vec = w
    tokens = grad.shape[1]
    grad_low = grad.astype(BF)
    for start in range(0, tokens, SPAN):
        at = slice(start, start + SPAN)
        for row in range(0, FF, CHUNK):
            rows = slice(row, row + CHUNK)
            grad_active = dot(down[rows], grad_low[:, at])
            kept["slope"][rows, at] = (grad_active * kept["slope"][rows, at].astype(F32)).astype(BF)
            yield
    unit_two = kept["unit_two"][...]
    normed = dot(up[...], kept["slope"][...])
    yield
    lane = lax.broadcasted_iota(jnp.int32, (tokens, D), 1)
    ones_lane = jnp.where(lane == 0, 1.0, 0.0).astype(BF)
    unit_two_rows = jnp.concatenate([flip(unit_two), ones_lane], axis=1)
    for row in range(0, FF, CHUNK):
        rows = slice(row, row + CHUNK)
        total["down"][rows] += dot(kept["active"][rows], grad_rows)
        yield
        total["up"][rows] += dot(kept["slope"][rows], unit_two_rows)
        yield
    total["down_bias"][...] += dot(jnp.ones((16, tokens), BF), grad_rows)[:8]
    return grad + norm_backward(normed, col(vec, FFN_GAIN), unit_two.astype(F32), kept["rows"][1:2])


def attend_backward(grad_middle, w, kept, total):
    qkv, proj, _, _, vec = w
    tokens = grad_middle.shape[1]
    blocks = tokens // BLOCK
    size = D // HEADS
    ones_row = jnp.ones((16, tokens), BF)
    lane = lax.broadcasted_iota(jnp.int32, (tokens, D), 1)
    grad_proj = grad_middle.astype(BF)
    attended = kept["attended"][...]
    total["proj"][...] += dot(jnp.concatenate([attended.astype(BF), ones_row], axis=0), flip(grad_proj))
    yield
    grad_attended = dot(proj[...], grad_proj).astype(BF).astype(F32)
    scaled = (grad_attended * head_spread(kept["rows"][2 : 2 + HEADS])).astype(BF)
    yield
    product = scaled.astype(F32) * attended
    centre = [jnp.sum(product[h * size : (h + 1) * size], axis=0, keepdims=True) for h in range(HEADS)]
    centre_high = [c.astype(BF).astype(F32) for c in centre]
    centre_low = [c - high for c, high in zip(centre, centre_high)]
    minus = jnp.where(lane < 2, -1.0, 0.0).astype(BF)
    value_rows = jnp.concatenate([flip(kept["value"][...]), minus], axis=1)
    key = kept["key"][...]
    query_rows = flip(kept["query"][...])
    scaled_rows = flip(scaled)
    grad_query = []
    grad_value = [None] * blocks
    grad_key = [None] * blocks

    def gather_row(parts, block, heads):
        return jnp.concatenate([parts[h][:, block * BLOCK : (block + 1) * BLOCK] for h in heads], axis=1)

    for block in range(blocks):
        seen = (block + 1) * BLOCK
        for pair, heads in enumerate(PAIRS):
            yield
            right = jnp.concatenate(
                [
                    head_columns(scaled, block, heads),
                    extra_rows([gather_row(centre_high, block, heads), gather_row(centre_low, block, heads)]),
                ],
                axis=0,
            )
            grad_probs = dot(value_rows[:seen], right)
            raised = kept["probs"][block][:, pair * len(heads) * BLOCK : (pair + 1) * len(heads) * BLOCK]
            grad_scores = raised * grad_probs.astype(BF)
            yield
            grad_query.append(own_columns(dot(key[:, :seen], grad_scores), heads))
            yield
            value_part = dot(raised, head_rows(scaled_rows, block, heads))
            for j in range(block + 1):
                v = value_part[j * BLOCK : (j + 1) * BLOCK]
                grad_value[j] = v if grad_value[j] is None else grad_value[j] + v
            yield
            key_part = dot(grad_scores, head_rows(query_rows, block, heads))
            for j in range(block + 1):
                k = key_part[j * BLOCK : (j + 1) * BLOCK]
                grad_key[j] = k if grad_key[j] is None else grad_key[j] + k
    yield
    grad_query = [jnp.concatenate(grad_query[len(PAIRS) * block : len(PAIRS) * (block + 1)], axis=0) for block in range(blocks)]
    grad_query = (jnp.concatenate(grad_query, axis=1) * size ** (-0.5)).astype(BF)
    grad_key = (jnp.concatenate(grad_key, axis=0) * math.log(2.0)).astype(BF)
    grad_value = jnp.concatenate(grad_value, axis=0).astype(BF)
    packed_rows = jnp.concatenate([flip(grad_query), grad_key, grad_value], axis=1)
    packed = jnp.concatenate([grad_query, flip(grad_key), flip(grad_value)], axis=0)
    yield
    unit = kept["unit"][...]
    total["qkv"][...] += dot(jnp.concatenate([unit, ones_row], axis=0), packed_rows)
    yield
    grad_normed = dot(qkv[...], packed)
    return grad_middle + norm_backward(grad_normed, col(vec, ATTN_GAIN), unit.astype(F32), kept["rows"][0:1])


def pack_grads(me, core, total, send):
    qkv, proj, up, down, down_bias = (total[n] for n in ("qkv", "proj", "up", "down", "down_bias"))
    up_t = [flip(up[D * part : D * (part + 1), :D]) for part in range(4)]
    up_sum = up[:, D:]
    up_sum_rows = [flip(up_sum[D * part : D * (part + 1)])[0:1] for part in range(4)]
    sums = jnp.concatenate(
        [
            qkv[D : D + 1, :D],
            qkv[D : D + 1, 2 * D : 3 * D],
            proj[D : D + 1],
            down_bias[0:1],
            jnp.zeros((D - 4, D), F32),
        ],
        axis=0,
    )
    columns = flip(sums)
    lane = lax.broadcasted_iota(jnp.int32, (8, 128), 1)
    whole = jnp.concatenate(
        [qkv[D : D + 1, D * part : D * (part + 1)] for part in range(3)]
        + up_sum_rows
        + [jnp.zeros((1, D), F32)],
        axis=0,
    )
    for owner in range(OWNERS):
        own = slice(8 * owner, 8 * owner + 8)
        small = jnp.where(lane < 4, columns[own], 0.0)
        for part in range(4):
            at = 32 * owner + 8 * part
            small = jnp.where(lane == 4 + part, jnp.broadcast_to(up_sum[at : at + 8, 0:1], (8, 128)), small)
        pieces = (
            [qkv[own, D * part : D * (part + 1)] for part in range(3)]
            + [proj[own]]
            + [u[own] for u in up_t]
            + [down[32 * owner : 32 * owner + 32], small, whole]
        )
        send[place_by(jnp.bitwise_xor(me, owner), core)] = jnp.concatenate(pieces, axis=0).astype(BF)


KEPT = ("unit", "query", "key", "value", "attended", "unit_two", "rows", "active", "slope")


def kept_shapes(tokens):
    shapes = {name: ((D, tokens), BF) for name in KEPT}
    shapes["rows"] = ((8, tokens), F32)
    shapes["attended"] = ((D, tokens), F32)
    shapes["active"] = ((FF, tokens), BF)
    shapes["slope"] = ((FF, tokens), BF)
    for block in range(tokens // BLOCK):
        shapes[f"probs{block}"] = (((block + 1) * BLOCK, HEADS * BLOCK), BF)
    return shapes


def as_kept(names, refs):
    kept = dict(zip(names, refs))
    probs = [kept.pop(n) for n in names if n.startswith("probs")]
    kept["probs"] = probs
    return kept


FORWARD_SCRATCH = [
    pltpu.VMEM((LAYERS, 3 * D, D), BF),
    pltpu.VMEM((LAYERS, D, D), BF),
    pltpu.VMEM((LAYERS, FF, D), BF),
    pltpu.VMEM((LAYERS, D, FF), BF),
]
BACKWARD_SCRATCH = [
    pltpu.VMEM((LAYERS, D, 3 * D), BF),
    pltpu.VMEM((LAYERS, D, D), BF),
    pltpu.VMEM((LAYERS, D, FF), BF),
    pltpu.VMEM((LAYERS, FF, D), BF),
]
VECTOR_SCRATCH = [
    pltpu.VMEM((LAYERS, OWNERS, SHARD_ROWS, 128), F32),
    pltpu.VMEM((LAYERS, D, 128), F32),
    pltpu.VMEM((LAYERS, OWNERS, 4, 8, 128), F32),
]
TOTALS = ("qkv", "proj", "up", "down", "down_bias")
TOTAL_SCRATCH = [
    pltpu.VMEM((LAYERS, D + 16, 3 * D), F32),
    pltpu.VMEM((LAYERS, D + 16, D), F32),
    pltpu.VMEM((LAYERS, FF, 2 * D), F32),
    pltpu.VMEM((LAYERS, FF, D), F32),
    pltpu.VMEM((LAYERS, 8, D), F32),
]


def key_bias_rows(field_row, length):
    tokens = field_row.shape[1]
    at = lax.broadcasted_iota(jnp.int32, (1, tokens), 1)
    shut = jnp.where(field_row == 0, NEGATIVE, jnp.where(at >= length, NEGATIVE, 0.0))
    place = lax.broadcasted_iota(jnp.int32, (16, tokens), 0)
    rows = jnp.where(place == 0, jnp.broadcast_to(shut, (16, tokens)), 0.0)
    columns = flip(rows)
    low = jnp.concatenate([columns, jnp.zeros((tokens, D - 16), F32)], axis=1).astype(BF)
    key_at = lax.broadcasted_iota(jnp.int32, (BLOCK, BLOCK), 0)
    query_at = lax.broadcasted_iota(jnp.int32, (BLOCK, BLOCK), 1)
    own = []
    for block in range(tokens // BLOCK):
        column = jnp.broadcast_to(columns[block * BLOCK : (block + 1) * BLOCK, 0:1], (BLOCK, BLOCK))
        own.append(jnp.where(key_at < query_at, column, jnp.where(key_at == query_at, 0.0, NEGATIVE)))
    return low, own


FORWARD_STEPS = (12, 8)
BACKWARD_STEPS = (10, 21)


def groups_of(seqs):
    sizes = [GROUP] * (seqs // GROUP)
    if seqs % GROUP:
        sizes.insert(max(len(sizes) - 1, 0), seqs % GROUP)
    ends = [sum(sizes[: g + 1]) for g in range(len(sizes))]
    return [list(range(end - size, end)) for end, size in zip(ends, sizes)]


def run_together(chains):
    results = [None] * len(chains)
    done = [0.0] * len(chains)
    rate = [[1.0 / steps for layer in range(LAYERS) for steps in phases for _ in range(steps)] for _, phases in chains]
    count = [0] * len(chains)
    live = list(range(len(chains)))
    while live:
        index = min(live, key=lambda i: done[i])
        try:
            next(chains[index][0])
            done[index] += rate[index][min(count[index], len(rate[index]) - 1)]
            count[index] += 1
        except StopIteration as stop:
            results[index] = stop.value
            live.remove(index)
    return results


def layers_kernel(
    names, known, again, length_ref, tokens_ref, field_ref, cot_ref, own_ref, other_ref, *rest
):
    if again:
        limits, outs, scratch = rest[0], rest[5:9], rest[9:]
        smallest, largest = jnp.min(limits[0:1]), jnp.max(limits[1:2])
        held = jnp.logical_and(smallest > 2.0**-60, largest < 2.0**60)
        pl.when(jnp.logical_not(held))(
            lambda: layers(
                names, known, None, length_ref, tokens_ref, field_ref, cot_ref, own_ref, other_ref, *outs, *scratch
            )
        )
    else:
        outs, limits, scratch = rest[:4], rest[4], rest[5:]
        limits[...] = jnp.ones(limits.shape, F32)
        layers(names, known, limits, length_ref, tokens_ref, field_ref, cot_ref, own_ref, other_ref, *outs, *scratch)


def layers(
    names, known, limits, length_ref, tokens_ref, field_ref, cot_ref, own_ref, other_ref, output_ref, grad_ref, keep_ref, away_ref, *scratch
):
    forward, backward, (stage, vec, up_bias) = scratch[:4], scratch[4:8], scratch[8:11]
    totals, kept = scratch[11:16], scratch[16:]
    seqs, tokens = field_ref.shape[0], field_ref.shape[2]
    me, core = position(known)
    unpack(me, core, own_ref, stage.at[core])
    unpack(me, 1 - core, other_ref, stage.at[1 - core])

    def total_of(layer):
        return dict(zip(TOTALS, [ref.at[layer] for ref in totals]))

    total = [total_of(layer) for layer in range(LAYERS)]
    for layer in range(LAYERS):
        unpack_forward(stage.at[layer], *[ref.at[layer] for ref in forward])
        unpack_backward(stage.at[layer], *[ref.at[layer] for ref in backward])
        unpack_vectors(stage.at[layer], vec.at[layer], up_bias.at[layer])

    def clear():
        for ref in totals:
            ref[...] = jnp.zeros_like(ref)

    def saved(slot, layer):
        n=len(names)
        return as_kept(names, [ref.at[layer] for ref in kept[slot*n:(slot+1)*n]])

    def rows_of(seq):
        return pl.ds(pl.multiple_of(seq * tokens, tokens), tokens)

    def forward_chain(seq, slot):
        bias, own_bias = key_bias_rows(field_ref[seq], length_ref[seq])
        state = flip(tokens_ref[rows_of(seq), :]).astype(F32)
        for layer in range(LAYERS):
            w = (*[ref.at[layer] for ref in forward], vec.at[layer], up_bias[layer].reshape(FF, 128))
            save = saved(slot, layer)
            yield from attend_forward(state, bias, own_bias, w, save, limits)
            yield
            state = yield from feed_forward(state, w, save)
            yield
        output_ref[rows_of(seq), :] = flip(state.astype(BF))

    def backward_chain(seq, slot):
        grad_rows = cot_ref[rows_of(seq), :]
        grad = flip(grad_rows).astype(F32)
        for layer in reversed(range(LAYERS)):
            w = (*[ref.at[layer] for ref in backward], vec.at[layer])
            save = saved(slot, layer)
            if layer < LAYERS - 1:
                grad_rows = flip(grad.astype(BF))
            grad = yield from feed_backward(grad, grad_rows, w, save, total[layer])
            yield
            grad = yield from attend_backward(grad, w, save, total[layer])
            yield
        grad_ref[rows_of(seq), :] = flip(grad)

    clear()
    if limits is None:

        def alone(seq, carry):
            run_together([(forward_chain(seq, 0), FORWARD_STEPS)])
            run_together([(backward_chain(seq, 0), BACKWARD_STEPS)])
            return carry

        lax.fori_loop(0, seqs, alone, 0)
    before = []
    for group in groups_of(seqs) + [[]] if limits is not None else []:
        used = [slot for _, slot in before]
        free = [slot for slot in range(2 * seqs) if slot not in used]
        now = list(zip(group, free))
        run_together(
            [(backward_chain(jnp.int32(seq), slot), BACKWARD_STEPS) for seq, slot in before]
            + [(forward_chain(jnp.int32(seq), slot), FORWARD_STEPS) for seq, slot in now]
        )
        before = now

    pack_grads(me, core, total_of(core), keep_ref)
    pack_grads(me, 1 - core, total_of(1 - core), away_ref)


def near(x):
    return pltpu.with_memory_space_constraint(x, pltpu.VMEM)


def far(x):
    return pltpu.with_memory_space_constraint(x, pltpu.HBM)


def run_layers(lengths, tokens, fields, cotangent, own, other, known):
    seqs, _, length = fields.shape
    shapes = kept_shapes(length)
    sizes = [len(group) for group in groups_of(seqs)]
    slots = max(a + b for a, b in zip(sizes, sizes[1:] + [0]))
    smem, vmem = pl.BlockSpec(memory_space=pltpu.SMEM), pl.BlockSpec(memory_space=pltpu.VMEM)
    send = pltpu.VMEM((OWNERS, GRAD_ROWS, 128), BF)
    tensors = (near(tokens), fields, near(cotangent), near(own), near(other))
    ranges = pltpu.VMEM((8, len(PAIRS[0]) * BLOCK), F32)
    outs = (pltpu.VMEM(tokens.shape, BF), pltpu.VMEM(tokens.shape, F32), send, send)

    def call(again, slots, *rest):
        return pl.pallas_call(
            functools.partial(layers_kernel, tuple(shapes), known, again),
            in_specs=[smem] + [vmem] * (5 + len(rest)),
            out_specs=[vmem] * (4 if again else 5),
            out_shape=outs if again else (*outs, ranges),
            input_output_aliases={7 + index: index for index in range(4)} if again else {},
            scratch_shapes=FORWARD_SCRATCH
            + BACKWARD_SCRATCH
            + VECTOR_SCRATCH
            + TOTAL_SCRATCH
            + [pltpu.VMEM((LAYERS, *shape), dtype) for _ in range(slots) for shape, dtype in shapes.values()],
            compiler_params=pltpu.CompilerParams(vmem_limit_bytes=AGAIN_VMEM_BYTES if again else VMEM_BYTES),
            name="layers_again" if again else "layers",
        )(lengths, *tensors, *rest)

    *results, limits = call(False, slots)
    return call(True, 1, near(limits), *(near(r) for r in results))


def pack_kernel(attn, qb, vb, proj, pb, ag, ash, up, ub, down, db, fg, fsh, shard_ref, own_ref):
    for layer in range(LAYERS):
        one = slice(layer, layer + 1)
        rows = [ref[one].astype(F32) for ref in (qb, vb, pb, ag, ash, db, fg, fsh)]
        bias = ub[one].astype(F32)
        rows += [bias[:, 8 * part : 8 * part + 8] for part in range(4)] + [jnp.zeros((4, 8), F32)]
        rows = jnp.concatenate(rows, axis=0)
        rows = jnp.concatenate([rows, jnp.zeros((16, 120), F32)], axis=1)
        small = flip(jnp.concatenate([rows, jnp.zeros((112, 128), F32)], axis=0))[:8]
        pieces = []
        for ref in (attn, proj, up):
            matrix = ref[layer].astype(F32)
            pieces += [matrix[:, 128 * part : 128 * (part + 1)] for part in range(matrix.shape[1] // 128)]
        shard_ref[layer] = jnp.concatenate(pieces + [down[layer].astype(F32), small], axis=0).astype(BF)
    own_ref[0] = shard_ref[lax.axis_index("dp")]


def run_pack(weights):
    vmem = pl.BlockSpec(memory_space=pltpu.VMEM)
    return pl.pallas_call(
        pack_kernel,
        in_specs=[vmem] * 13,
        out_specs=[vmem] * 2,
        out_shape=[
            jax.ShapeDtypeStruct((LAYERS, SHARD_ROWS, 128), BF),
            pltpu.VMEM((1, SHARD_ROWS, 128), BF),
        ],
        name="pack",
    )(*weights)


def finish_kernel(own_ref, other_ref, shard_ref, *outs):
    (attn, query_bias, value_bias, proj, proj_bias, attn_gain, attn_shift, up, up_bias, down, down_bias, ffn_gain, ffn_shift) = outs
    lane = lax.broadcasted_iota(jnp.int32, (8, 128), 1)
    for layer in range(LAYERS):
        red = jnp.where(lax.axis_index("dp") == layer, own_ref[...], other_ref[...])
        own = shard_ref[layer].astype(F32)
        small_in = own[96:104]
        small, whole = red[96:104], red[104:112]
        gains = [None, None]
        shifts = [None, None]
        for index, (places, gain_at, shift_at, target) in enumerate(
            (((0, 8, 16), ATTN_GAIN, ATTN_SHIFT, attn), ((32, 40, 48, 56), FFN_GAIN, FFN_SHIFT, up))
        ):
            gain, shift = small_in[:, gain_at : gain_at + 1], small_in[:, shift_at : shift_at + 1]
            first = 0 if index == 0 else 3
            gain_sum = jnp.zeros((8, 128), F32)
            shift_sum = jnp.zeros((8, 128), F32)
            for part, place in enumerate(places):
                grad, weight = red[place : place + 8], own[place : place + 8]
                column_sum = whole[first + part : first + part + 1]
                target[layer, :, 128 * part : 128 * (part + 1)] = gain * grad + shift * column_sum
                gain_sum += weight * grad
                shift_sum += weight * column_sum
            gains[index] = jnp.sum(gain_sum, axis=1, keepdims=True)
            shifts[index] = jnp.sum(shift_sum, axis=1, keepdims=True)
        proj[layer] = red[24:32]
        down[layer] = red[64:96]
        for at, column in ((8, gains[0]), (9, shifts[0]), (10, gains[1]), (11, shifts[1])):
            small = jnp.where(lane == at, jnp.broadcast_to(column, (8, 128)), small)
        rows = flip(small)
        query_bias[layer : layer + 1] = rows[0:1]
        value_bias[layer : layer + 1] = rows[1:2]
        proj_bias[layer : layer + 1] = rows[2:3]
        down_bias[layer : layer + 1] = rows[3:4]
        up_bias[layer : layer + 1] = jnp.concatenate([rows[4 + part : 5 + part] for part in range(4)], axis=1)
        attn_gain[layer : layer + 1] = rows[8:9]
        attn_shift[layer : layer + 1] = rows[9:10]
        ffn_gain[layer : layer + 1] = rows[10:11]
        ffn_shift[layer : layer + 1] = rows[11:12]


def run_finish(own, other, shard):
    layers = LAYERS
    vector = jax.ShapeDtypeStruct((layers, 8), F32)

    def matrix(rows, columns):
        return jax.ShapeDtypeStruct((layers, rows, columns), F32)

    shapes = [
        matrix(8, 3 * D), vector, vector, matrix(8, D), vector, vector, vector, matrix(8, FF),
        jax.ShapeDtypeStruct((layers, 32), F32), matrix(32, D), vector, vector, vector,
    ]
    return pl.pallas_call(
        finish_kernel,
        in_specs=[pl.BlockSpec(memory_space=pltpu.VMEM)] * 3,
        out_specs=[pl.BlockSpec(memory_space=pltpu.VMEM)] * len(shapes),
        out_shape=shapes,
        name="finish",
    )(near(own), near(other), shard)


def pack_weights(weights, layer, owners):
    attn, qb, vb, proj, pb, ag, ash, up, ub, down, db, fg, fsh = (w[layer] for w in weights)

    def blocks(matrix, count):
        return [matrix[:, 128 * part : 128 * (part + 1)].reshape(owners, 8, 128) for part in range(count)]

    vectors = [v.reshape(owners, 8, 1) for v in (qb, vb, pb, ag, ash, db, fg, fsh)]
    bias = jnp.swapaxes(ub.reshape(owners, 4, 8), 1, 2)
    small = jnp.concatenate(vectors + [bias], axis=2)
    small = jnp.pad(small, ((0, 0), (0, 0), (0, 128 - small.shape[2])))
    return jnp.concatenate(
        blocks(attn, 3) + blocks(proj, 1) + blocks(up, 4) + [down.reshape(owners, 32, 128), small], axis=1
    )


def exchange(x, step):
    pairs = [
        (core * OWNERS + i, core * OWNERS + (i ^ bits[step])) for core, bits in enumerate(STEP_BITS) for i in range(OWNERS)
    ]
    return lax.ppermute(x, ("dp", "wide"), pairs)


def swap_cores(x):
    return lax.ppermute(x, "dp", [(0, 1), (1, 0)])


def gather_doubling(own):
    held = jnp.zeros((OWNERS, *own.shape[1:]), own.dtype)
    held = lax.dynamic_update_slice_in_dim(held, own, 0, 0)
    for step in range(4):
        count = 1 << step
        if step == 3:
            other = swap_cores(held[:count])
        arrived = exchange(held[:count], step)
        held = lax.dynamic_update_slice_in_dim(held, arrived, count, 0)
    other = jnp.concatenate([other, swap_cores(arrived)], axis=0)
    return held, other


def reduce_halving(keep, away, beside):
    held = keep.astype(F32) + swap_cores(away).astype(F32)
    for step in (3, 2, 1, 0):
        count = 1 << step
        arrived = exchange(held[count:].astype(BF), step)
        if step == 3:
            arrived, *beside = lax.optimization_barrier((arrived, *(far(x) for x in beside)))
        held = held[:count] + arrived.astype(F32)
    return held[0], beside


def reduce_general(send, weights, gathered, layer):
    total = jnp.stack([send[place_of(owner, layer)] for owner in range(OWNERS)]).astype(F32)

    def matrix(places):
        return jnp.concatenate([total[:, p : p + 8].reshape(D, 128) for p in places], axis=1)

    attn, up, proj = matrix((0, 8, 16)), matrix((32, 40, 48, 56)), matrix((24,))
    down = total[:, 64:96].reshape(FF, D)
    small, whole = total[:, 96:104].reshape(D, 128), total[0, 104:112]
    attn_w, up_w = gathered[0][layer].astype(F32), gathered[7][layer].astype(F32)
    again, ashift, fgain, fshift = (gathered[i][layer].astype(F32)[:, None] for i in (5, 6, 11, 12))
    attn_sum, up_sum = whole[0:3].reshape(1, 3 * D), whole[3:7].reshape(1, FF)
    up_bias = jnp.swapaxes(total[:, 96:104, 4:8], 1, 2).reshape(FF)
    local = (
        again * attn + ashift * attn_sum, small[:, 0], small[:, 1], proj, small[:, 2],
        jnp.sum(attn_w * attn, axis=1), jnp.sum(attn_w * attn_sum, axis=1),
        fgain * up + fshift * up_sum, up_bias, down, small[:, 3],
        jnp.sum(up_w * up, axis=1), jnp.sum(up_w * up_sum, axis=1),
    )
    return tuple(
        lax.psum_scatter(lax.psum(g, "dp"), "wide", scatter_dimension=0, tiled=True) for g in local
    )


def body(tokens, field_ids, seq_lengths, cotangent, *weights, owners):
    seqs = seq_lengths.shape[0]
    fields = field_ids.reshape(seqs, 1, -1)
    doubling = owners == OWNERS
    if doubling:
        shard, own = run_pack(weights)
        own, other = gather_doubling(own)
    else:
        gathered = [lax.all_gather(w, "wide", axis=1, tiled=True) for w in weights]
        packed = [pack_weights(gathered, layer, OWNERS) for layer in range(LAYERS)]
        places = [sorted(range(OWNERS), key=lambda owner: place_of(owner, core)) for core in range(2)]
        own, other = (jnp.stack([p[owner] for owner in order]) for p, order in zip(packed, places))
    output, token_grad, keep, away = run_layers(seq_lengths, tokens, fields, cotangent, own, other, doubling)
    if doubling:
        reduced, (output, token_grad) = reduce_halving(keep, away, (output, token_grad))
        grads = run_finish(reduced, swap_cores(reduced), shard)
    else:
        by_layer = [reduce_general(send, weights, gathered, layer) for layer, send in enumerate((keep, away))]
        grads = [jnp.stack(pair) for pair in zip(*by_layer)]
    return (output, token_grad, *grads)


def solution(mesh):
    rows, vector = P(("dp", "wide"), None), P(("dp", "wide"))
    flat, square = P(None, "wide"), P(None, "wide", None)
    params = (square, flat, flat, square, flat, flat, flat, square, flat, square, flat, flat, flat)
    return jax.shard_map(
        functools.partial(body, owners=mesh.shape["wide"]),
        mesh=mesh,
        in_specs=(rows, vector, vector, rows, *params),
        out_specs=(rows, rows, *params),
        check_vma=False,
    )
```

```python
import functools
import math

import jax
import jax.numpy as jnp
from jax import lax
from jax.experimental import pallas as pl
from jax.experimental.pallas import tpu as pltpu
from jax.sharding import PartitionSpec as P

HEADS = 4
EPSILON = 1e-05
NEGATIVE = -1e30
BLOCK = 128
D = 128
FF = 512
OWNERS = 16
SHARD_ROWS = 104
GRAD_ROWS = 112
LAYERS = 2
GROUP = 2
SPAN = 256
CHUNK = 256
VMEM_BYTES = 50 * 2**20
AGAIN_VMEM_BYTES = 36 * 2**20

BF = jnp.bfloat16
F32 = jnp.float32
NN = (((1,), (0,)), ((), ()))


def dot(a, b):
    return lax.dot_general(a, b, NN, preferred_element_type=F32)


def flip(x):
    return jnp.transpose(x)


def col(vec_ref, index):
    return vec_ref[:, index : index + 1]


STEP_BITS = ((8, 4, 2, 1), (4, 8, 1, 2))


def place_of(relative, core):
    first = ((relative & 1) << 3) | ((relative & 2) << 1) | ((relative & 4) >> 1) | ((relative & 8) >> 3)
    return first if core == 0 else ((first & 5) << 1) | ((first & 10) >> 1)


def place_by(relative, core):
    return jnp.where(core == 0, place_of(relative, 0), place_of(relative, 1))


def position(known):
    return (lax.axis_index("wide"), lax.axis_index("dp")) if known else (jnp.int32(0), jnp.int32(0))


def unpack(me, core, packed_ref, stage):
    for owner in range(OWNERS):
        stage[owner] = packed_ref[place_by(jnp.bitwise_xor(me, owner), core)].astype(F32)


def stage_rows(stage, start, count):
    return stage[:, start : start + count, :].reshape(OWNERS * count, 128)


def unpack_forward(stage, qkv_t, proj_t, up_t, down_t):
    for part in range(3):
        qkv_t[part * D : (part + 1) * D, :] = flip(stage_rows(stage, 8 * part, 8)).astype(BF)
    proj_t[...] = flip(stage_rows(stage, 24, 8)).astype(BF)
    for part in range(4):
        up_t[part * D : (part + 1) * D, :D] = flip(stage_rows(stage, 32 + 8 * part, 8)).astype(BF)
    down_t[...] = flip(stage_rows(stage, 64, 32)).astype(BF)


def unpack_backward(stage, qkv, proj, up, down):
    for part in range(3):
        qkv[:, part * D : (part + 1) * D] = stage_rows(stage, 8 * part, 8).astype(BF)
    proj[...] = stage_rows(stage, 24, 8).astype(BF)
    for part in range(4):
        up[:, part * D : (part + 1) * D] = stage_rows(stage, 32 + 8 * part, 8).astype(BF)
    down[...] = stage_rows(stage, 64, 32).astype(BF)


def unpack_vectors(stage, vec, up_bias, up_t):
    small = stage[:, 96:104, :]
    vec[...] = small.reshape(D, 128)
    lane = lax.broadcasted_iota(jnp.int32, (OWNERS, 8, 128), 2)
    for part in range(4):
        piece = jnp.broadcast_to(small[:, :, 8 + part : 9 + part], (OWNERS, 8, 128))
        up_bias[:, part, :, :] = jnp.where(lane == 0, piece, 0.0)
    up_t[:, D:] = up_bias[...].reshape(FF, 128).astype(BF)


QUERY_BIAS, VALUE_BIAS, PROJ_BIAS, ATTN_GAIN, ATTN_SHIFT, DOWN_BIAS, FFN_GAIN, FFN_SHIFT = range(8)


def norm_stats(x):
    mean = jnp.mean(x, axis=0, keepdims=True)
    centred = x - mean
    spread = jnp.mean(centred * centred, axis=0, keepdims=True)
    rstd = lax.rsqrt(spread + EPSILON)
    return centred * rstd, rstd


def norm_backward(grad_out, gain, unit, rstd):
    weighted = grad_out * gain
    first = jnp.mean(weighted, axis=0, keepdims=True)
    second = jnp.mean(weighted * unit, axis=0, keepdims=True)
    return rstd * (weighted - first - unit * second)


def head_columns(x, block, heads):
    size = D // HEADS
    piece = x[:, block * BLOCK : (block + 1) * BLOCK]
    columns = []
    for head in heads:
        rows = [
            piece[head * size : (head + 1) * size] if other == head else jnp.zeros((size, BLOCK), piece.dtype)
            for other in range(HEADS)
        ]
        columns.append(jnp.concatenate(rows, axis=0))
    return jnp.concatenate(columns, axis=1)


def head_rows(x, block, heads):
    size = D // HEADS
    piece = x[block * BLOCK : (block + 1) * BLOCK, :]
    lane = lax.broadcasted_iota(jnp.int32, (BLOCK, D), 1) // size
    return jnp.concatenate([jnp.where(lane == head, piece, jnp.zeros_like(piece)) for head in heads], axis=0)


def own_columns(x, heads):
    size = D // HEADS
    return jnp.concatenate(
        [x[head * size : (head + 1) * size, at * BLOCK : (at + 1) * BLOCK] for at, head in enumerate(heads)], axis=0
    )


def head_spread(rows):
    size = D // HEADS
    return jnp.concatenate(
        [jnp.broadcast_to(rows[head : head + 1], (size, rows.shape[1])) for head in range(HEADS)], axis=0
    )


def extra_rows(rows, total=D):
    width = rows[0].shape[1]
    filled = jnp.zeros((16, width), F32)
    place = lax.broadcasted_iota(jnp.int32, (16, width), 0)
    for index, row in enumerate(rows):
        filled = jnp.where(place == index, jnp.broadcast_to(row, (16, width)), filled)
    return jnp.concatenate([filled.astype(BF), jnp.zeros((total - 16, width), BF)], axis=0)


PAIRS = ((0, 1, 2, 3),)


def attend_forward(x, key_bias, own_bias, w, save, limits):
    qkv_t, _, _, _, vec = w
    tokens = x.shape[1]
    blocks = tokens // BLOCK
    size = D // HEADS
    unit, rstd = norm_stats(x)
    normed = (unit * col(vec, ATTN_GAIN) + col(vec, ATTN_SHIFT)).astype(BF)
    save["unit"][...] = unit.astype(BF)
    save["rows"][0:1] = rstd
    yield
    factor = size ** (-0.5) / math.log(2.0)
    query = ((dot(qkv_t[:D], normed) + col(vec, QUERY_BIAS)) * factor).astype(BF)
    save["query"][...] = query
    yield
    key = dot(qkv_t[D : 2 * D], normed).astype(BF)
    save["key"][...] = key
    key_plain = flip(key)
    key_rows = jnp.concatenate([key_plain, key_bias], axis=1)
    yield
    value = (dot(qkv_t[2 * D :], normed) + col(vec, VALUE_BIAS)).astype(BF)
    save["value"][...] = value
    value_ones = jnp.concatenate([value, jnp.ones((16, tokens), BF)], axis=0)
    ones = extra_rows([jnp.ones((1, len(PAIRS[0]) * BLOCK), F32)])
    for block in range(blocks):
        seen = (block + 1) * BLOCK
        at = slice(block * BLOCK, seen)
        for pair, heads in enumerate(PAIRS):
            yield
            columns = head_columns(query, block, heads)
            scores = dot(key_plain[seen - BLOCK : seen], columns) + jnp.concatenate([own_bias[block]] * len(heads), axis=1)
            if block:
                right = jnp.concatenate([columns, ones], axis=0)
                scores = jnp.concatenate([dot(key_rows[: seen - BLOCK], right), scores], axis=0)
            if limits is None:
                scores = scores - jnp.max(scores, axis=0, keepdims=True)
            raised = jnp.exp2(scores).astype(BF)
            save["probs"][block][:, pair * len(heads) * BLOCK : (pair + 1) * len(heads) * BLOCK] = raised
            yield
            summed = dot(value_ones[:, :seen], raised)
            total = summed[D : D + 1]
            if limits is not None:
                limits[0:1] = jnp.minimum(limits[0:1], total)
                limits[1:2] = jnp.maximum(limits[1:2], total)
            inv = 1.0 / total
            for place, head in enumerate(heads):
                save["rows"][2 + head : 3 + head, at] = inv[:, place * BLOCK : (place + 1) * BLOCK]
            save["attended"][heads[0] * size : (heads[-1] + 1) * size, at] = own_columns(summed[:D] * inv, heads)


def feed_forward(x, w, save):
    _, proj_t, up_t, down_t, vec = w
    tokens = x.shape[1]
    middle = x + (dot(proj_t[...], save["attended"][...].astype(BF)) + col(vec, PROJ_BIAS))
    yield
    unit_two, rstd_two = norm_stats(middle)
    save["unit_two"][...] = unit_two.astype(BF)
    save["rows"][1:2] = rstd_two
    normed_two = (unit_two * col(vec, FFN_GAIN) + col(vec, FFN_SHIFT)).astype(BF)
    normed_two = jnp.concatenate([normed_two, extra_rows([jnp.ones((1, tokens), F32)])], axis=0)
    root = math.sqrt(2.0 / math.pi)
    result = []
    for start in range(0, tokens, SPAN):
        at = slice(start, start + SPAN)
        for row in range(0, FF, CHUNK):
            yield
            rows = slice(row, row + CHUNK)
            expanded = dot(up_t[rows], normed_two[:, at])
            square = expanded * expanded
            bent = jnp.tanh(expanded * (root + (root * 0.044715) * square))
            half = 0.5 + 0.5 * bent
            active = expanded * half
            save["active"][rows, at] = active.astype(BF)
            slope = half + active * ((1.0 - bent) * (root + (3.0 * root * 0.044715) * square))
            save["slope"][rows, at] = slope.astype(BF)
        yield
        result.append(middle[:, at] + col(vec, DOWN_BIAS) + dot(down_t[...], save["active"][:, at]))
    return jnp.concatenate(result, axis=1)


def feed_backward(grad, grad_rows, w, kept, total):
    _, _, up, down, vec = w
    tokens = grad.shape[1]
    grad_low = grad.astype(BF)
    for start in range(0, tokens, SPAN):
        at = slice(start, start + SPAN)
        for row in range(0, FF, CHUNK):
            rows = slice(row, row + CHUNK)
            grad_active = dot(down[rows], grad_low[:, at])
            kept["slope"][rows, at] = (grad_active * kept["slope"][rows, at].astype(F32)).astype(BF)
            yield
    unit_two = kept["unit_two"][...]
    normed = dot(up[...], kept["slope"][...])
    yield
    lane = lax.broadcasted_iota(jnp.int32, (tokens, D), 1)
    ones_lane = jnp.where(lane == 0, 1.0, 0.0).astype(BF)
    unit_two_rows = jnp.concatenate([flip(unit_two), ones_lane], axis=1)
    for row in range(0, FF, CHUNK):
        rows = slice(row, row + CHUNK)
        total["down"][rows] += dot(kept["active"][rows], grad_rows)
        yield
        total["up"][rows] += dot(kept["slope"][rows], unit_two_rows)
        yield
    total["down_bias"][...] += dot(jnp.ones((16, tokens), BF), grad_rows)[:8]
    return grad + norm_backward(normed, col(vec, FFN_GAIN), unit_two.astype(F32), kept["rows"][1:2])


def attend_backward(grad_middle, w, kept, total):
    qkv, proj, _, _, vec = w
    tokens = grad_middle.shape[1]
    blocks = tokens // BLOCK
    size = D // HEADS
    ones_row = jnp.ones((16, tokens), BF)
    lane = lax.broadcasted_iota(jnp.int32, (tokens, D), 1)
    grad_proj = grad_middle.astype(BF)
    attended = kept["attended"][...]
    total["proj"][...] += dot(jnp.concatenate([attended.astype(BF), ones_row], axis=0), flip(grad_proj))
    yield
    grad_attended = dot(proj[...], grad_proj).astype(BF).astype(F32)
    scaled = (grad_attended * head_spread(kept["rows"][2 : 2 + HEADS])).astype(BF)
    yield
    product = scaled.astype(F32) * attended
    centre = [jnp.sum(product[h * size : (h + 1) * size], axis=0, keepdims=True) for h in range(HEADS)]
    centre_high = [c.astype(BF).astype(F32) for c in centre]
    centre_low = [c - high for c, high in zip(centre, centre_high)]
    minus = jnp.where(lane < 2, -1.0, 0.0).astype(BF)
    value_rows = jnp.concatenate([flip(kept["value"][...]), minus], axis=1)
    key = kept["key"][...]
    query_rows = flip(kept["query"][...])
    scaled_rows = flip(scaled)
    grad_query = []
    grad_value = [None] * blocks
    grad_key = [None] * blocks

    def gather_row(parts, block, heads):
        return jnp.concatenate([parts[h][:, block * BLOCK : (block + 1) * BLOCK] for h in heads], axis=1)

    for block in range(blocks):
        seen = (block + 1) * BLOCK
        for pair, heads in enumerate(PAIRS):
            yield
            right = jnp.concatenate(
                [
                    head_columns(scaled, block, heads),
                    extra_rows([gather_row(centre_high, block, heads), gather_row(centre_low, block, heads)]),
                ],
                axis=0,
            )
            grad_probs = dot(value_rows[:seen], right)
            raised = kept["probs"][block][:, pair * len(heads) * BLOCK : (pair + 1) * len(heads) * BLOCK]
            grad_scores = raised * grad_probs.astype(BF)
            yield
            grad_query.append(own_columns(dot(key[:, :seen], grad_scores), heads))
            value_part = dot(raised, head_rows(scaled_rows, block, heads))
            for j in range(block + 1):
                v = value_part[j * BLOCK : (j + 1) * BLOCK]
                grad_value[j] = v if grad_value[j] is None else grad_value[j] + v
            key_part = dot(grad_scores, head_rows(query_rows, block, heads))
            for j in range(block + 1):
                k = key_part[j * BLOCK : (j + 1) * BLOCK]
                grad_key[j] = k if grad_key[j] is None else grad_key[j] + k
    yield
    grad_query = [jnp.concatenate(grad_query[len(PAIRS) * block : len(PAIRS) * (block + 1)], axis=0) for block in range(blocks)]
    grad_query = (jnp.concatenate(grad_query, axis=1) * size ** (-0.5)).astype(BF)
    grad_key = (jnp.concatenate(grad_key, axis=0) * math.log(2.0)).astype(BF)
    grad_value = jnp.concatenate(grad_value, axis=0).astype(BF)
    packed_rows = jnp.concatenate([flip(grad_query), grad_key, grad_value], axis=1)
    packed = jnp.concatenate([grad_query, flip(grad_key), flip(grad_value)], axis=0)
    yield
    unit = kept["unit"][...]
    total["qkv"][...] += dot(jnp.concatenate([unit, ones_row], axis=0), packed_rows)
    yield
    grad_normed = dot(qkv[...], packed)
    return grad_middle + norm_backward(grad_normed, col(vec, ATTN_GAIN), unit.astype(F32), kept["rows"][0:1])


def pack_grads(me, core, total, send):
    qkv, proj, up, down, down_bias = (total[n] for n in ("qkv", "proj", "up", "down", "down_bias"))
    up_t = [flip(up[D * part : D * (part + 1), :D]) for part in range(4)]
    up_sum = up[:, D:]
    up_sum_rows = [flip(up_sum[D * part : D * (part + 1)])[0:1] for part in range(4)]
    sums = jnp.concatenate(
        [
            qkv[D : D + 1, :D],
            qkv[D : D + 1, 2 * D : 3 * D],
            proj[D : D + 1],
            down_bias[0:1],
            jnp.zeros((D - 4, D), F32),
        ],
        axis=0,
    )
    columns = flip(sums)
    lane = lax.broadcasted_iota(jnp.int32, (8, 128), 1)
    whole = jnp.concatenate(
        [qkv[D : D + 1, D * part : D * (part + 1)] for part in range(3)]
        + up_sum_rows
        + [jnp.zeros((1, D), F32)],
        axis=0,
    )
    for owner in range(OWNERS):
        own = slice(8 * owner, 8 * owner + 8)
        small = jnp.where(lane < 4, columns[own], 0.0)
        for part in range(4):
            at = 32 * owner + 8 * part
            small = jnp.where(lane == 4 + part, jnp.broadcast_to(up_sum[at : at + 8, 0:1], (8, 128)), small)
        pieces = (
            [qkv[own, D * part : D * (part + 1)] for part in range(3)]
            + [proj[own]]
            + [u[own] for u in up_t]
            + [down[32 * owner : 32 * owner + 32], small, whole]
        )
        send[place_by(jnp.bitwise_xor(me, owner), core)] = jnp.concatenate(pieces, axis=0).astype(BF)


KEPT = ("unit", "query", "key", "value", "attended", "unit_two", "rows", "active", "slope")


def kept_shapes(tokens):
    shapes = {name: ((D, tokens), BF) for name in KEPT}
    shapes["rows"] = ((8, tokens), F32)
    shapes["attended"] = ((D, tokens), F32)
    shapes["active"] = ((FF, tokens), BF)
    shapes["slope"] = ((FF, tokens), BF)
    for block in range(tokens // BLOCK):
        shapes[f"probs{block}"] = (((block + 1) * BLOCK, HEADS * BLOCK), BF)
    return shapes


def as_kept(names, refs):
    kept = dict(zip(names, refs))
    probs = [kept.pop(n) for n in names if n.startswith("probs")]
    kept["probs"] = probs
    return kept


FORWARD_SCRATCH = [
    pltpu.VMEM((LAYERS, 3 * D, D), BF),
    pltpu.VMEM((LAYERS, D, D), BF),
    pltpu.VMEM((LAYERS, FF, 2 * D), BF),
    pltpu.VMEM((LAYERS, D, FF), BF),
]
BACKWARD_SCRATCH = [
    pltpu.VMEM((LAYERS, D, 3 * D), BF),
    pltpu.VMEM((LAYERS, D, D), BF),
    pltpu.VMEM((LAYERS, D, FF), BF),
    pltpu.VMEM((LAYERS, FF, D), BF),
]
VECTOR_SCRATCH = [
    pltpu.VMEM((LAYERS, OWNERS, SHARD_ROWS, 128), F32),
    pltpu.VMEM((LAYERS, D, 128), F32),
    pltpu.VMEM((LAYERS, OWNERS, 4, 8, 128), F32),
]
TOTALS = ("qkv", "proj", "up", "down", "down_bias")
TOTAL_SCRATCH = [
    pltpu.VMEM((LAYERS, D + 16, 3 * D), F32),
    pltpu.VMEM((LAYERS, D + 16, D), F32),
    pltpu.VMEM((LAYERS, FF, 2 * D), F32),
    pltpu.VMEM((LAYERS, FF, D), F32),
    pltpu.VMEM((LAYERS, 8, D), F32),
]


def key_bias_rows(field_row, length):
    tokens = field_row.shape[1]
    at = lax.broadcasted_iota(jnp.int32, (1, tokens), 1)
    shut = jnp.where(field_row == 0, NEGATIVE, jnp.where(at >= length, NEGATIVE, 0.0))
    place = lax.broadcasted_iota(jnp.int32, (16, tokens), 0)
    rows = jnp.where(place == 0, jnp.broadcast_to(shut, (16, tokens)), 0.0)
    columns = flip(rows)
    low = jnp.concatenate([columns, jnp.zeros((tokens, D - 16), F32)], axis=1).astype(BF)
    key_at = lax.broadcasted_iota(jnp.int32, (BLOCK, BLOCK), 0)
    query_at = lax.broadcasted_iota(jnp.int32, (BLOCK, BLOCK), 1)
    own = []
    for block in range(tokens // BLOCK):
        column = jnp.broadcast_to(columns[block * BLOCK : (block + 1) * BLOCK, 0:1], (BLOCK, BLOCK))
        own.append(jnp.where(key_at < query_at, column, jnp.where(key_at == query_at, 0.0, NEGATIVE)))
    return low, own


FORWARD_STEPS = (12, 8)
BACKWARD_STEPS = (10, 13)
PREPARE_STEPS = (9,)


def groups_of(seqs):
    sizes = [GROUP] * (seqs // GROUP)
    if seqs % GROUP:
        sizes.insert(max(len(sizes) - 1, 0), seqs % GROUP)
    ends = [sum(sizes[: g + 1]) for g in range(len(sizes))]
    return [list(range(end - size, end)) for end, size in zip(ends, sizes)]


def run_together(chains):
    results = [None] * len(chains)
    done = [0.0] * len(chains)
    rate = [[1.0 / steps for layer in range(LAYERS) for steps in phases for _ in range(steps)] for _, phases in chains]
    count = [0] * len(chains)
    live = list(range(len(chains)))
    while live:
        index = min(live, key=lambda i: done[i])
        try:
            next(chains[index][0])
            done[index] += rate[index][min(count[index], len(rate[index]) - 1)]
            count[index] += 1
        except StopIteration as stop:
            results[index] = stop.value
            live.remove(index)
    return results


def layers_kernel(
    names, known, again, length_ref, tokens_ref, field_ref, cot_ref, own_ref, other_ref, *rest
):
    if again:
        limits, outs, scratch = rest[0], rest[5:9], rest[9:]
        smallest, largest = jnp.min(limits[0:1]), jnp.max(limits[1:2])
        held = jnp.logical_and(smallest > 2.0**-60, largest < 2.0**60)
        pl.when(jnp.logical_not(held))(
            lambda: layers(
                names, known, None, length_ref, tokens_ref, field_ref, cot_ref, own_ref, other_ref, *outs, *scratch
            )
        )
    else:
        outs, limits, scratch = rest[:4], rest[4], rest[5:]
        limits[...] = jnp.ones(limits.shape, F32)
        layers(names, known, limits, length_ref, tokens_ref, field_ref, cot_ref, own_ref, other_ref, *outs, *scratch)


def layers(
    names, known, limits, length_ref, tokens_ref, field_ref, cot_ref, own_ref, other_ref, output_ref, grad_ref, keep_ref, away_ref, *scratch
):
    forward, backward, (stage, vec, up_bias) = scratch[:4], scratch[4:8], scratch[8:11]
    totals, kept = scratch[11:16], scratch[16:]
    seqs, tokens = field_ref.shape[0], field_ref.shape[2]
    me, core = position(known)
    unpack(me, core, own_ref, stage.at[core])
    unpack(me, 1 - core, other_ref, stage.at[1 - core])

    def total_of(layer):
        return dict(zip(TOTALS, [ref.at[layer] for ref in totals]))

    total = [total_of(layer) for layer in range(LAYERS)]

    def unpack_layer(layer):
        unpack_forward(stage.at[layer], *[ref.at[layer] for ref in forward])
        unpack_vectors(stage.at[layer], vec.at[layer], up_bias.at[layer], forward[2].at[layer])

    def prepare():
        for layer in range(1, LAYERS):
            unpack_layer(layer)
            yield
        for layer in range(LAYERS):
            unpack_backward(stage.at[layer], *[ref.at[layer] for ref in backward])
            yield
        for ref in totals:
            ref[...] = jnp.zeros_like(ref)
            yield

    unpack_layer(0)

    def saved(slot, layer):
        n=len(names)
        return as_kept(names, [ref.at[layer] for ref in kept[slot*n:(slot+1)*n]])

    def rows_of(seq):
        return pl.ds(pl.multiple_of(seq * tokens, tokens), tokens)

    def forward_chain(seq, slot):
        bias, own_bias = key_bias_rows(field_ref[seq], length_ref[seq])
        state = flip(tokens_ref[rows_of(seq), :]).astype(F32)
        for layer in range(LAYERS):
            w = (*[ref.at[layer] for ref in forward], vec.at[layer])
            save = saved(slot, layer)
            yield from attend_forward(state, bias, own_bias, w, save, limits)
            yield
            state = yield from feed_forward(state, w, save)
            yield
        output_ref[rows_of(seq), :] = flip(state.astype(BF))

    def backward_chain(seq, slot):
        grad_rows = cot_ref[rows_of(seq), :]
        grad = flip(grad_rows).astype(F32)
        for layer in reversed(range(LAYERS)):
            w = (*[ref.at[layer] for ref in backward], vec.at[layer])
            save = saved(slot, layer)
            if layer < LAYERS - 1:
                grad_rows = flip(grad.astype(BF))
            grad = yield from feed_backward(grad, grad_rows, w, save, total[layer])
            yield
            grad = yield from attend_backward(grad, w, save, total[layer])
            yield
        grad_ref[rows_of(seq), :] = flip(grad)

    if limits is None:
        run_together([(prepare(), PREPARE_STEPS)])

        def alone(seq, carry):
            run_together([(forward_chain(seq, 0), FORWARD_STEPS)])
            run_together([(backward_chain(seq, 0), BACKWARD_STEPS)])
            return carry

        lax.fori_loop(0, seqs, alone, 0)
    before = []
    for group in groups_of(seqs) + [[]] if limits is not None else []:
        used = [slot for _, slot in before]
        free = [slot for slot in range(2 * seqs) if slot not in used]
        now = list(zip(group, free))
        run_together(
            [(backward_chain(jnp.int32(seq), slot), BACKWARD_STEPS) for seq, slot in before]
            + [(forward_chain(jnp.int32(seq), slot), FORWARD_STEPS) for seq, slot in now]
            + ([] if before else [(prepare(), PREPARE_STEPS)])
        )
        before = now

    pack_grads(me, core, total_of(core), keep_ref)
    pack_grads(me, 1 - core, total_of(1 - core), away_ref)


def near(x):
    return pltpu.with_memory_space_constraint(x, pltpu.VMEM)


def far(x):
    return pltpu.with_memory_space_constraint(x, pltpu.HBM)


def run_layers(lengths, tokens, fields, cotangent, own, other, known):
    seqs, _, length = fields.shape
    shapes = kept_shapes(length)
    sizes = [len(group) for group in groups_of(seqs)]
    slots = max(a + b for a, b in zip(sizes, sizes[1:] + [0]))
    smem, vmem = pl.BlockSpec(memory_space=pltpu.SMEM), pl.BlockSpec(memory_space=pltpu.VMEM)
    send = pltpu.VMEM((OWNERS, GRAD_ROWS, 128), BF)
    tensors = (near(tokens), fields, near(cotangent), near(own), near(other))
    ranges = pltpu.VMEM((8, len(PAIRS[0]) * BLOCK), F32)
    outs = (pltpu.VMEM(tokens.shape, BF), pltpu.VMEM(tokens.shape, F32), send, send)

    def call(again, slots, *rest):
        return pl.pallas_call(
            functools.partial(layers_kernel, tuple(shapes), known, again),
            in_specs=[smem] + [vmem] * (5 + len(rest)),
            out_specs=[vmem] * (4 if again else 5),
            out_shape=outs if again else (*outs, ranges),
            input_output_aliases={7 + index: index for index in range(4)} if again else {},
            scratch_shapes=FORWARD_SCRATCH
            + BACKWARD_SCRATCH
            + VECTOR_SCRATCH
            + TOTAL_SCRATCH
            + [pltpu.VMEM((LAYERS, *shape), dtype) for _ in range(slots) for shape, dtype in shapes.values()],
            compiler_params=pltpu.CompilerParams(vmem_limit_bytes=AGAIN_VMEM_BYTES if again else VMEM_BYTES),
            name="layers_again" if again else "layers",
        )(lengths, *tensors, *rest)

    *results, limits = call(False, slots)
    return call(True, 1, near(limits), *(near(r) for r in results))


def pack_kernel(attn, qb, vb, proj, pb, ag, ash, up, ub, down, db, fg, fsh, shard_ref, own_ref):
    for layer in range(LAYERS):
        one = slice(layer, layer + 1)
        rows = [ref[one].astype(F32) for ref in (qb, vb, pb, ag, ash, db, fg, fsh)]
        bias = ub[one].astype(F32)
        rows += [bias[:, 8 * part : 8 * part + 8] for part in range(4)] + [jnp.zeros((4, 8), F32)]
        rows = jnp.concatenate(rows, axis=0)
        rows = jnp.concatenate([rows, jnp.zeros((16, 120), F32)], axis=1)
        small = flip(jnp.concatenate([rows, jnp.zeros((112, 128), F32)], axis=0))[:8]
        pieces = []
        for ref in (attn, proj, up):
            matrix = ref[layer].astype(F32)
            pieces += [matrix[:, 128 * part : 128 * (part + 1)] for part in range(matrix.shape[1] // 128)]
        shard_ref[layer] = jnp.concatenate(pieces + [down[layer].astype(F32), small], axis=0).astype(BF)
    own_ref[0] = shard_ref[lax.axis_index("dp")]


def run_pack(weights):
    vmem = pl.BlockSpec(memory_space=pltpu.VMEM)
    return pl.pallas_call(
        pack_kernel,
        in_specs=[vmem] * 13,
        out_specs=[vmem] * 2,
        out_shape=[
            jax.ShapeDtypeStruct((LAYERS, SHARD_ROWS, 128), BF),
            pltpu.VMEM((1, SHARD_ROWS, 128), BF),
        ],
        name="pack",
    )(*weights)


def finish_kernel(own_ref, other_ref, shard_ref, *outs):
    (attn, query_bias, value_bias, proj, proj_bias, attn_gain, attn_shift, up, up_bias, down, down_bias, ffn_gain, ffn_shift) = outs
    lane = lax.broadcasted_iota(jnp.int32, (8, 128), 1)
    for layer in range(LAYERS):
        red = jnp.where(lax.axis_index("dp") == layer, own_ref[...], other_ref[...])
        own = shard_ref[layer].astype(F32)
        small_in = own[96:104]
        small, whole = red[96:104], red[104:112]
        gains = [None, None]
        shifts = [None, None]
        for index, (places, gain_at, shift_at, target) in enumerate(
            (((0, 8, 16), ATTN_GAIN, ATTN_SHIFT, attn), ((32, 40, 48, 56), FFN_GAIN, FFN_SHIFT, up))
        ):
            gain, shift = small_in[:, gain_at : gain_at + 1], small_in[:, shift_at : shift_at + 1]
            first = 0 if index == 0 else 3
            gain_sum = jnp.zeros((8, 128), F32)
            shift_sum = jnp.zeros((8, 128), F32)
            for part, place in enumerate(places):
                grad, weight = red[place : place + 8], own[place : place + 8]
                column_sum = whole[first + part : first + part + 1]
                target[layer, :, 128 * part : 128 * (part + 1)] = gain * grad + shift * column_sum
                gain_sum += weight * grad
                shift_sum += weight * column_sum
            gains[index] = jnp.sum(gain_sum, axis=1, keepdims=True)
            shifts[index] = jnp.sum(shift_sum, axis=1, keepdims=True)
        proj[layer] = red[24:32]
        down[layer] = red[64:96]
        for at, column in ((8, gains[0]), (9, shifts[0]), (10, gains[1]), (11, shifts[1])):
            small = jnp.where(lane == at, jnp.broadcast_to(column, (8, 128)), small)
        rows = flip(small)
        query_bias[layer : layer + 1] = rows[0:1]
        value_bias[layer : layer + 1] = rows[1:2]
        proj_bias[layer : layer + 1] = rows[2:3]
        down_bias[layer : layer + 1] = rows[3:4]
        up_bias[layer : layer + 1] = jnp.concatenate([rows[4 + part : 5 + part] for part in range(4)], axis=1)
        attn_gain[layer : layer + 1] = rows[8:9]
        attn_shift[layer : layer + 1] = rows[9:10]
        ffn_gain[layer : layer + 1] = rows[10:11]
        ffn_shift[layer : layer + 1] = rows[11:12]


def run_finish(own, other, shard):
    layers = LAYERS
    vector = jax.ShapeDtypeStruct((layers, 8), F32)

    def matrix(rows, columns):
        return jax.ShapeDtypeStruct((layers, rows, columns), F32)

    shapes = [
        matrix(8, 3 * D), vector, vector, matrix(8, D), vector, vector, vector, matrix(8, FF),
        jax.ShapeDtypeStruct((layers, 32), F32), matrix(32, D), vector, vector, vector,
    ]
    return pl.pallas_call(
        finish_kernel,
        in_specs=[pl.BlockSpec(memory_space=pltpu.VMEM)] * 3,
        out_specs=[pl.BlockSpec(memory_space=pltpu.VMEM)] * len(shapes),
        out_shape=shapes,
        name="finish",
    )(near(own), near(other), shard)


def pack_weights(weights, layer, owners):
    attn, qb, vb, proj, pb, ag, ash, up, ub, down, db, fg, fsh = (w[layer] for w in weights)

    def blocks(matrix, count):
        return [matrix[:, 128 * part : 128 * (part + 1)].reshape(owners, 8, 128) for part in range(count)]

    vectors = [v.reshape(owners, 8, 1) for v in (qb, vb, pb, ag, ash, db, fg, fsh)]
    bias = jnp.swapaxes(ub.reshape(owners, 4, 8), 1, 2)
    small = jnp.concatenate(vectors + [bias], axis=2)
    small = jnp.pad(small, ((0, 0), (0, 0), (0, 128 - small.shape[2])))
    return jnp.concatenate(
        blocks(attn, 3) + blocks(proj, 1) + blocks(up, 4) + [down.reshape(owners, 32, 128), small], axis=1
    )


def exchange(x, step):
    pairs = [
        (core * OWNERS + i, core * OWNERS + (i ^ bits[step])) for core, bits in enumerate(STEP_BITS) for i in range(OWNERS)
    ]
    return lax.ppermute(x, ("dp", "wide"), pairs)


def swap_cores(x):
    return lax.ppermute(x, "dp", [(0, 1), (1, 0)])


def gather_doubling(own):
    held = jnp.zeros((OWNERS, *own.shape[1:]), own.dtype)
    held = lax.dynamic_update_slice_in_dim(held, own, 0, 0)
    for step in range(4):
        count = 1 << step
        if step == 3:
            other = swap_cores(held[:count])
        arrived = exchange(held[:count], step)
        held = lax.dynamic_update_slice_in_dim(held, arrived, count, 0)
    other = jnp.concatenate([other, swap_cores(arrived)], axis=0)
    return held, other


def reduce_halving(keep, away, beside):
    held = keep.astype(F32) + swap_cores(away).astype(F32)
    for step in (3, 2, 1, 0):
        count = 1 << step
        arrived = exchange(held[count:].astype(BF), step)
        if step == 3:
            arrived, *beside = lax.optimization_barrier((arrived, *(far(x) for x in beside)))
        held = held[:count] + arrived.astype(F32)
    return held[0], beside


def reduce_general(send, weights, gathered, layer):
    total = jnp.stack([send[place_of(owner, layer)] for owner in range(OWNERS)]).astype(F32)

    def matrix(places):
        return jnp.concatenate([total[:, p : p + 8].reshape(D, 128) for p in places], axis=1)

    attn, up, proj = matrix((0, 8, 16)), matrix((32, 40, 48, 56)), matrix((24,))
    down = total[:, 64:96].reshape(FF, D)
    small, whole = total[:, 96:104].reshape(D, 128), total[0, 104:112]
    attn_w, up_w = gathered[0][layer].astype(F32), gathered[7][layer].astype(F32)
    again, ashift, fgain, fshift = (gathered[i][layer].astype(F32)[:, None] for i in (5, 6, 11, 12))
    attn_sum, up_sum = whole[0:3].reshape(1, 3 * D), whole[3:7].reshape(1, FF)
    up_bias = jnp.swapaxes(total[:, 96:104, 4:8], 1, 2).reshape(FF)
    local = (
        again * attn + ashift * attn_sum, small[:, 0], small[:, 1], proj, small[:, 2],
        jnp.sum(attn_w * attn, axis=1), jnp.sum(attn_w * attn_sum, axis=1),
        fgain * up + fshift * up_sum, up_bias, down, small[:, 3],
        jnp.sum(up_w * up, axis=1), jnp.sum(up_w * up_sum, axis=1),
    )
    return tuple(
        lax.psum_scatter(lax.psum(g, "dp"), "wide", scatter_dimension=0, tiled=True) for g in local
    )


def body(tokens, field_ids, seq_lengths, cotangent, *weights, owners):
    seqs = seq_lengths.shape[0]
    fields = field_ids.reshape(seqs, 1, -1)
    doubling = owners == OWNERS
    if doubling:
        shard, own = run_pack(weights)
        own, other = gather_doubling(own)
    else:
        gathered = [lax.all_gather(w, "wide", axis=1, tiled=True) for w in weights]
        packed = [pack_weights(gathered, layer, OWNERS) for layer in range(LAYERS)]
        places = [sorted(range(OWNERS), key=lambda owner: place_of(owner, core)) for core in range(2)]
        own, other = (jnp.stack([p[owner] for owner in order]) for p, order in zip(packed, places))
    output, token_grad, keep, away = run_layers(seq_lengths, tokens, fields, cotangent, own, other, doubling)
    if doubling:
        reduced, (output, token_grad) = reduce_halving(keep, away, (output, token_grad))
        grads = run_finish(reduced, swap_cores(reduced), shard)
    else:
        by_layer = [reduce_general(send, weights, gathered, layer) for layer, send in enumerate((keep, away))]
        grads = [jnp.stack(pair) for pair in zip(*by_layer)]
    return (output, token_grad, *grads)


def solution(mesh):
    rows, vector = P(("dp", "wide"), None), P(("dp", "wide"))
    flat, square = P(None, "wide"), P(None, "wide", None)
    params = (square, flat, flat, square, flat, flat, flat, square, flat, square, flat, flat, flat)
    return jax.shard_map(
        functools.partial(body, owners=mesh.shape["wide"]),
        mesh=mesh,
        in_specs=(rows, vector, vector, rows, *params),
        out_specs=(rows, rows, *params),
        check_vma=False,
    )
```
